512 devices in a mesh: dp: 8 (over z), vocab: 64 (over x, y, core).
Axes of the slice: x: 4, y: 8, z: 8, core: 2. Of those that a mesh axis runs over, the one named last changes fastest.
Arguments:
- hidden_ref: bfloat16 [1280, 4096], P('dp'), may hold values from -640 to 640
- hidden_train: bfloat16 [1280, 4096], P('dp'), may hold values from -640 to 640
- head_ref: bfloat16 [64512, 4096], P('vocab', 'dp'), may hold values from -1 to 1
- head_train: bfloat16 [64512, 4096], P('vocab', 'dp'), may hold values from -1 to 1
- targets: int32 [1280], P('dp'), may hold values from 0 to 64511
- mask: int32 [1280], P('dp'), may hold values from 0 to 1, as said below
Outputs:
- excess: float32 [1280], P('dp')
- loss_value: float32 [], replicated
- hidden_grad: float32 [4096, 1280], P('vocab', 'dp')
The draws below stay inside these ranges and needn't reach their ends.
Inputs may be any that keep to these rules, and one draw needn't show every extreme that they name: `mask`: exactly 100 ones in each aligned block of 160 tokens.
All inputs are finite; a program needn't handle non-finite values.
Results may differ from the reference program's by a relative error of at most 0.0016.
Values may be sent and summed in bfloat16 or wider, within the bound.
A program may use at most 64 MiB of HBM per device.

```python
import math
import jax
import jax.numpy as jnp
import numpy as np
from jax import lax

D = 4096
VROWS = 1008
TOK_DEV = 160
SEL_DEV = 100
VOCAB = 64512
TOKENS = 1280
SELECTED = 800
N_VOCAB = 64


def draw_hidden_ref(key, part):
    key = jax.random.fold_in(key, 11)
    first_key, second_key = jax.random.split(key, 2)
    row_index = jnp.arange(TOKENS)
    base_values = jnp.clip(jax.random.normal(first_key, (TOKENS, D), jnp.float32), -6.0, 6.0)
    row_scale = jnp.exp(jax.random.uniform(second_key, (TOKENS, 1), jnp.float32, 0.0, math.log(4.0)))
    row_scale = row_scale * (1.0 + 2.0 * row_index[:, None] / TOKENS)
    values = base_values * row_scale
    return values.astype(jnp.bfloat16)


def draw_hidden_train(key, part):
    key = jax.random.fold_in(key, 12)
    first_key, second_key = jax.random.split(key, 2)
    row_index = jnp.arange(TOKENS)
    base_values = jnp.clip(jax.random.normal(first_key, (TOKENS, D), jnp.float32), -6.0, 6.0)
    row_scale = jnp.exp(jax.random.uniform(second_key, (TOKENS, 1), jnp.float32, 0.0, math.log(4.0)))
    row_scale = row_scale * (1.0 + 2.0 * row_index[:, None] / TOKENS)
    values = base_values * row_scale
    return values.astype(jnp.bfloat16)


def draw_head_ref(key, part):
    key = jax.random.fold_in(key, 13)
    first_key, second_key = jax.random.split(key, 2)
    row_scale = jnp.exp(jax.random.uniform(second_key, (VOCAB, 1), jnp.float32, math.log(0.5), math.log(2.0))) * (3.0 / math.sqrt(D))
    base_values = jnp.clip(jax.random.normal(first_key, (VOCAB, D), jnp.float32), -6.0, 6.0) * row_scale
    return jnp.clip(base_values, -1.0, 1.0).astype(jnp.bfloat16)


def draw_head_train(key, part):
    key = jax.random.fold_in(key, 14)
    first_key, second_key = jax.random.split(key, 2)
    row_scale = jnp.exp(jax.random.uniform(second_key, (VOCAB, 1), jnp.float32, math.log(0.5), math.log(2.0))) * (3.0 / math.sqrt(D))
    base_values = jnp.clip(jax.random.normal(first_key, (VOCAB, D), jnp.float32), -6.0, 6.0) * row_scale
    return jnp.clip(base_values, -1.0, 1.0).astype(jnp.bfloat16)


def draw_mask(key, part):
    key = jax.random.fold_in(key, 7)
    raw_scores = jax.random.randint(key, (TOKENS,), 0, 1048576) * TOK_DEV + jnp.arange(TOKENS, dtype=jnp.int32) % TOK_DEV
    blocked = raw_scores.reshape(TOKENS // TOK_DEV, TOK_DEV)
    ranks = jnp.argsort(jnp.argsort(blocked, axis=1), axis=1)
    return (ranks < SEL_DEV).astype(jnp.int32).reshape(TOKENS)


def with_ends(values, rng, low, high):
    spot = [jax.random.randint(jax.random.fold_in(rng, axis), (), 0, length) for axis, length in enumerate(values.shape)]
    longest = values.shape.index(max(values.shape))
    neighbour = spot[:longest] + [(spot[longest] + 1) % values.shape[longest]] + spot[longest + 1:]
    return values.at[tuple(spot)].set(low).at[tuple(neighbour)].set(high)


def rank_bounds(amount, skew):
    weights = [(1 << 20) // math.isqrt(grade ** skew) + 1 for grade in range(1, amount + 1)]
    width = 1 + sum(weights) // (1 << 30)
    return np.cumsum(np.array([max(1, weight // width) for weight in weights]))


def skewed_ids(stream_key, dims, count, slope):
    grid = rank_bounds(count, slope)
    lot = jax.random.randint(jax.random.fold_in(stream_key, 1), dims, 0, int(grid[count - 1]))
    rank = jnp.searchsorted(jnp.asarray(grid, jnp.int32), lot, side="right")
    return jax.random.permutation(jax.random.fold_in(stream_key, 2), count)[rank].astype(jnp.int32)


def setup_inputs(seed: int = 0) -> dict:
    key_of = jax.random.split(jax.random.key(seed), 7)
    return {
        "hidden_ref": draw_hidden_ref(jax.random.fold_in(key_of[6], 71), 0),
        "hidden_train": draw_hidden_train(jax.random.fold_in(key_of[6], 71), 0),
        "head_ref": draw_head_ref(jax.random.fold_in(key_of[6], 71), 0),
        "head_train": draw_head_train(jax.random.fold_in(key_of[6], 71), 0),
        "targets": with_ends(skewed_ids(key_of[4], (TOKENS,), VOCAB, 2), jax.random.fold_in(key_of[4], 3), 0, VOCAB - 1).astype(jnp.int32),
        "mask": draw_mask(jax.random.fold_in(key_of[6], 71), 0),
    }


loss_scale = 64.0


def block_logits(hidden, weight_block):
    return jnp.dot(hidden.astype(jnp.float32), weight_block.astype(jnp.float32).T, precision=lax.Precision.HIGHEST)


def head_stats(hidden, weight, targets):
    blocks = weight.reshape(N_VOCAB, VROWS, D)
    offsets = jnp.arange(N_VOCAB, dtype=jnp.int32) * VROWS
    columns = jnp.arange(VROWS, dtype=jnp.int32)

    def advance(carry, inputs):
        run_max, run_sum, picked = carry
        weight_block, offset = inputs
        logits = block_logits(hidden, weight_block)
        new_max = jnp.maximum(run_max, jnp.max(logits, axis=1))
        run_sum = run_sum * jnp.exp(run_max - new_max) + jnp.sum(jnp.exp(logits - new_max[:, None]), axis=1)
        target_hit = (columns[None, :] + offset) == targets[:, None]
        picked = picked + jnp.sum(jnp.where(target_hit, logits, 0.0), axis=1)
        return (new_max, run_sum, picked), None

    start_state = (jnp.full((TOKENS,), -jnp.inf, jnp.float32), jnp.zeros((TOKENS,), jnp.float32), jnp.zeros((TOKENS,), jnp.float32))
    final_state, unused = lax.scan(advance, start_state, (blocks, offsets))
    return final_state


def reference(hidden_ref, hidden_train, head_ref, head_train, targets, mask):
    ref_max, ref_sum, ref_pick = head_stats(hidden_ref, head_ref, targets)
    train_max, train_sum, train_pick = head_stats(hidden_train, head_train, targets)
    ce_ref = jnp.log(ref_sum) + ref_max - ref_pick
    ce_train = jnp.log(train_sum) + train_max - train_pick
    excess = ce_train - ce_ref
    select_weight = mask.astype(jnp.float32)
    loss_value = jnp.sum(select_weight * ce_train) / SELECTED
    blocks = head_train.reshape(N_VOCAB, VROWS, D)
    offsets = jnp.arange(N_VOCAB, dtype=jnp.int32) * VROWS
    columns = jnp.arange(VROWS, dtype=jnp.int32)

    def accumulate(grad_sum, inputs):
        weight_block, offset = inputs
        logits = block_logits(hidden_train, weight_block)
        probabilities = jnp.exp(logits - train_max[:, None]) / train_sum[:, None]
        target_hit = ((columns[None, :] + offset) == targets[:, None]).astype(jnp.float32)
        logit_grads = (loss_scale * select_weight[:, None] * (probabilities - target_hit)).astype(jnp.bfloat16)
        grad_sum = grad_sum + jnp.dot(weight_block.astype(jnp.float32).T, logit_grads.astype(jnp.float32).T, precision=lax.Precision.HIGHEST)
        return grad_sum, None

    hidden_grad, unused = lax.scan(accumulate, jnp.zeros((D, TOKENS), jnp.float32), (blocks, offsets))
    return excess, loss_value, hidden_grad
```

```python
import functools

import jax
import jax.numpy as jnp
from jax import lax
from jax.experimental import pallas as pl
from jax.experimental.pallas import tpu as pltpu
from jax.sharding import PartitionSpec as P

MESH = pl.DeviceIdType.MESH
NX, NY, NZ = 4, 8, 8
loss_scale = 64.0
TOK = 160
SEL = 100
SLOT = 112
ROWS = 128
PIECE = 128
FEAT = 512
FAR_FIRST = (4, 3, 5, 2, 6, 1, 7)
NEAR_FIRST = (1, 7, 2, 6, 3, 5, 4)


def coords():
    z = lax.axis_index("dp")
    v = lax.axis_index("vocab")
    return v // 16, (v // 2) % NY, z, v % 2


def vocab_index(x, y, c):
    return (x * NY + y) * 2 + c


def greet(devices):
    barrier = pltpu.get_barrier_semaphore()
    for device in devices:
        pl.semaphore_signal(barrier, inc=1, device_id=device, device_id_type=MESH)
    pl.semaphore_wait(barrier, len(devices))


def remote(src, dst, send_sem, recv_sem, device):
    return pltpu.make_async_remote_copy(
        src_ref=src, dst_ref=dst, send_sem=send_sem, recv_sem=recv_sem,
        device_id=device, device_id_type=MESH,
    )


class Ring:
    def __init__(self, buf, pos, size, width, right, left, active, send_sem, recv_sem):
        self.buf, self.pos, self.size, self.width = buf, pos, size, width
        self.devices = (right, left)
        self.active, self.send_sem, self.recv_sem = active, send_sem, recv_sem

    def copy(self, step, way, slot, arriving):
        back = step if arriving else step - 1
        sign = -1 if way == 0 else 1
        block = (self.pos + sign * back + self.size) % self.size
        column = pl.multiple_of(block * self.width, self.width)
        part = self.buf.at[pl.ds(TOK * slot, TOK), pl.ds(column, self.width)]
        return remote(
            part, part, self.send_sem.at[step - 1, way, slot],
            self.recv_sem.at[step - 1, way, slot], self.devices[way],
        )

    def ways(self, step, slot):
        if 2 * step < self.size:
            return (0, 1)
        return (0,) if slot < 2 else (1,)

    def send(self, step, slot):
        @pl.when(self.active(slot))
        def _():
            for way in self.ways(step, slot):
                self.copy(step, way, slot, False).start()

    def wait(self, step, slot):
        @pl.when(self.active(slot))
        def _():
            for way in self.ways(step, slot):
                self.copy(step, way, slot, True).wait_recv()

    def drain(self):
        for slot in range(4):
            @pl.when(self.active(slot))
            def _():
                for step in range(1, self.size // 2 + 1):
                    for way in self.ways(step, slot):
                        self.copy(step, way, slot, False).wait_send()


def spread_kernel(
    hid_ref, hid_train, head_ref, head_train, meta,
    x_ref, x_train, g_ref, g_train, meta_all,
    local_sem, z_send, z_recv, m_send, m_recv, w_send, w_recv, s_send, s_recv,
    ra_send, ra_recv, rb_send, rb_recv, ta_send, ta_recv, tb_send, tb_recv,
):
    x, y, z, c = coords()
    v = vocab_index(x, y, c)
    sibling = (z, vocab_index(x, y, 1 - c))
    x_right = (z, vocab_index((x + 1) % NX, y, c))
    x_left = (z, vocab_index((x + NX - 1) % NX, y, c))
    y_right = (z, vocab_index(x, (y + 1) % NY, c))
    y_left = (z, vocab_index(x, (y + NY - 1) % NY, c))
    peers = {s: ((z + s) % NZ, v) for s in range(1, NZ)}
    greet([peers[s] for s in range(1, NZ)] + [sibling, x_right, x_left, y_right, y_left])

    own_slot = z % 4
    is_source = z // 4 == c

    def active(slot):
        return z != 4 * c + slot

    hid = (hid_ref, hid_train)
    wide = (x_ref, x_train)
    heads = (head_ref, head_train)
    got = (g_ref, g_train)
    piece_at = (
        pl.multiple_of((y * NX + x) * PIECE, PIECE),
        pl.multiple_of((x * NY + y) * PIECE, PIECE),
    )

    def z_copy(a, slot, s):
        return remote(
            hid[a].at[:, pl.ds(piece_at[a], PIECE)],
            wide[a].at[pl.ds(pl.multiple_of(TOK * slot, 16), TOK), pl.ds(piece_at[a], PIECE)],
            z_send.at[a, s - 1], z_recv.at[a, slot], peers[s],
        )

    def own_copy(a):
        return pltpu.make_async_copy(
            hid[a],
            wide[a].at[pl.ds(pl.multiple_of(TOK * own_slot, 16), TOK), :],
            local_sem.at[a],
        )

    @pl.when(is_source)
    def _():
        for a in (1, 0):
            for s in FAR_FIRST:
                z_copy(a, own_slot, s).start()
        for a in (0, 1):
            own_copy(a).start()

    def meta_copy(s, arriving):
        source = (z + NZ - s) % NZ if arriving else z
        return remote(
            meta, meta_all.at[source], m_send.at[s - 1], m_recv.at[s - 1], peers[s]
        )

    own_meta = pltpu.make_async_copy(meta, meta_all.at[z], local_sem.at[2])
    own_meta.start()
    for s in range(1, NZ):
        meta_copy(s, False).start()

    def row_block(j):
        return pl.multiple_of(j * ROWS - 16 * (j // 7), 16)

    mine = pl.ds(pl.multiple_of(ROWS * c, ROWS), ROWS)

    def part_of(a, source):
        return got[a].at[mine, pl.ds(pl.multiple_of(source * FEAT, FEAT), FEAT)]

    def head_copy(a, s, arriving):
        dest = (z + s) % NZ
        source = (z + NZ - s) % NZ if arriving else z
        return remote(
            heads[a].at[pl.ds(row_block(dest), ROWS), :], part_of(a, source),
            w_send.at[a, s - 1], w_recv.at[a, s - 1], peers[s],
        )

    def share_copy(a, s):
        part = part_of(a, (z + NZ - s) % NZ)
        return remote(part, part, s_send.at[a, s], s_recv.at[a, s], sibling)

    def share_arriving(a, s):
        source = (z + NZ - s) % NZ
        part = got[a].at[
            pl.ds(pl.multiple_of(ROWS * (1 - c), ROWS), ROWS),
            pl.ds(pl.multiple_of(source * FEAT, FEAT), FEAT),
        ]
        return remote(part, part, s_send.at[a, s], s_recv.at[a, s], sibling)

    own_rows = [
        pltpu.make_async_copy(
            heads[a].at[pl.ds(row_block(z), ROWS), :], part_of(a, z), local_sem.at[3 + a]
        )
        for a in (0, 1)
    ]
    for a in (1, 0):
        own_rows[a].start()
        for s in FAR_FIRST:
            head_copy(a, s, False).start()

    ra = Ring(x_ref, y * NX + x, NX, PIECE, x_right, x_left, active, ra_send, ra_recv)
    rb = Ring(x_ref, y, NY, NX * PIECE, y_right, y_left, active, rb_send, rb_recv)
    ta = Ring(x_train, x * NY + y, NY, PIECE, y_right, y_left, active, ta_send, ta_recv)
    tb = Ring(x_train, x, NX, NY * PIECE, x_right, x_left, active, tb_send, tb_recv)
    ra_base, ta_base = y * NX, x * NY
    ra.pos, ta.pos = x, y

    def first_stage(ring, base):
        def copy(step, way, slot, arriving):
            back = step if arriving else step - 1
            sign = -1 if way == 0 else 1
            block = base + (ring.pos + sign * back + ring.size) % ring.size
            part = ring.buf.at[
                pl.ds(TOK * slot, TOK), pl.ds(pl.multiple_of(block * PIECE, PIECE), PIECE)
            ]
            return remote(
                part, part, ring.send_sem.at[step - 1, way, slot],
                ring.recv_sem.at[step - 1, way, slot], ring.devices[way],
            )
        ring.copy = copy

    first_stage(ra, ra_base)
    first_stage(ta, ta_base)

    slots = range(4)
    for slot in slots:
        for a, ring in ((1, ta), (0, ra)):
            @pl.when(active(slot))
            def _():
                z_copy(a, slot, 1).wait_recv()
            ring.send(1, slot)

    def advance(*moves):
        for slot in slots:
            for ring, step, after, after_step in moves:
                ring.wait(step, slot)
                if after is not None:
                    after.send(after_step, slot)

    advance((ta, 1, ta, 2), (ra, 1, ra, 2))
    advance((ta, 2, ta, 3), (ra, 2, rb, 1))
    advance((ta, 3, ta, 4))
    advance((ta, 4, tb, 1))
    for a in (1, 0):
        own_rows[a].wait()
        share_copy(a, 0).start()
    advance((rb, 1, rb, 2))
    for s in (1, 7, 2, 6):
        head_copy(1, s, True).wait_recv()
        share_copy(1, s).start()
    advance((rb, 2, rb, 3), (tb, 1, tb, 2))
    for s in (3, 5, 4):
        head_copy(1, s, True).wait_recv()
        share_copy(1, s).start()
    advance((rb, 3, rb, 4))
    for s in NEAR_FIRST:
        head_copy(0, s, True).wait_recv()
        share_copy(0, s).start()
    advance((tb, 2, None, 0), (rb, 4, None, 0))

    own_meta.wait()
    for s in range(1, NZ):
        meta_copy(s, True).wait_recv()
    for a in (1, 0):
        for s in range(NZ):
            share_arriving(a, s).wait_recv()

    @pl.when(is_source)
    def _():
        for a in (0, 1):
            own_copy(a).wait()
            for s in range(1, NZ):
                z_copy(a, own_slot, s).wait_send()

    for s in range(1, NZ):
        meta_copy(s, False).wait_send()
    for a in (0, 1):
        for s in range(1, NZ):
            head_copy(a, s, False).wait_send()
        for s in range(NZ):
            share_copy(a, s).wait_send()
    for ring in (ra, rb, ta, tb):
        ring.drain()


def spread(hidden_ref, hidden_train, head_ref, head_train, meta):
    anywhere = pl.BlockSpec(memory_space=pl.ANY)
    dma = pltpu.SemaphoreType.DMA
    half = 4 * TOK
    width = hidden_ref.shape[1]
    sds = jax.ShapeDtypeStruct
    return pl.pallas_call(
        spread_kernel,
        out_shape=[
            sds((half, width), jnp.bfloat16), sds((half, width), jnp.bfloat16),
            sds((2 * ROWS, width), jnp.bfloat16), sds((2 * ROWS, width), jnp.bfloat16),
            sds((NZ,) + meta.shape, meta.dtype),
        ],
        in_specs=[anywhere] * 5,
        out_specs=[anywhere] * 5,
        scratch_shapes=[
            dma((5,)), dma((2, NZ - 1)), dma((2, 4)), dma((NZ - 1,)), dma((NZ - 1,)),
            dma((2, NZ - 1)), dma((2, NZ - 1)), dma((2, NZ)), dma((2, NZ)),
            dma((2, 2, 4)), dma((2, 2, 4)), dma((4, 2, 4)), dma((4, 2, 4)),
            dma((4, 2, 4)), dma((4, 2, 4)), dma((2, 2, 4)), dma((2, 2, 4)),
        ],
        compiler_params=pltpu.CompilerParams(collective_id=0, has_side_effects=True),
        name="spread",
    )(hidden_ref, hidden_train, head_ref, head_train, meta)


def merge(blocks):
    out = []
    for base in (0, 3):
        tops = [b[base:base + 1, :] for b in blocks]
        top = functools.reduce(jnp.maximum, tops)
        total = sum(b[base + 1:base + 2, :] * jnp.exp(t - top) for b, t in zip(blocks, tops))
        picked = sum(b[base + 2:base + 3, :] for b in blocks)
        out += [top, total, picked]
    return out


def stats_kernel(mine, out, acc, zbuf, xbuf, ybuf, z_send, z_recv, x_send, x_recv,
                 y_send, y_recv, c_send, c_recv):
    x, y, z, c = coords()
    v = vocab_index(x, y, c)
    sibling = (z, vocab_index(x, y, 1 - c))
    z_peers = [((z + s) % NZ, v) for s in range(1, NZ)]
    x_peers = [(z, vocab_index((x + s) % NX, y, c)) for s in range(1, NX)]
    y_peers = [(z, vocab_index(x, (y + s) % NY, c)) for s in range(1, NY)]
    greet(z_peers + x_peers + y_peers + [sibling])

    source = mine
    level = 0
    pending = []
    for peers, buf, send, recv in (
        (z_peers, zbuf, z_send, z_recv),
        (x_peers, xbuf, x_send, x_recv),
        (y_peers, ybuf, y_send, y_recv),
    ):
        copies = [
            remote(source, buf.at[s], send.at[s], recv.at[s], peer)
            for s, peer in enumerate(peers)
        ]
        for copy in copies:
            copy.start()
        for copy in copies:
            copy.wait_recv()
        parts = merge([source[...]] + [buf[s] for s in range(len(peers))])
        if level < 2:
            target = acc.at[level]
            for row, part in enumerate(parts):
                target[row:row + 1, :] = part
            target[6:8, :] = jnp.zeros_like(target[6:8, :])
            source = target
        pending += copies
        level += 1
    for row, part in enumerate(parts):
        out[c, row:row + 1, :] = part
    out[c, 6:8, :] = jnp.zeros((2, mine.shape[1]), jnp.float32)
    share = remote(out.at[c], out.at[c], c_send, c_recv, sibling)
    share.start()
    remote(out.at[1 - c], out.at[1 - c], c_send, c_recv, sibling).wait_recv()
    share.wait_send()
    for copy in pending:
        copy.wait_send()


def exchange_stats(stats):
    vmem = pl.BlockSpec(memory_space=pltpu.VMEM)
    dma = pltpu.SemaphoreType.DMA
    shape = stats.shape
    return pl.pallas_call(
        stats_kernel,
        out_shape=jax.ShapeDtypeStruct((2,) + shape, jnp.float32),
        in_specs=[vmem],
        out_specs=vmem,
        scratch_shapes=[
            pltpu.VMEM((2,) + shape, jnp.float32), pltpu.VMEM((NZ - 1,) + shape, jnp.float32),
            pltpu.VMEM((NX - 1,) + shape, jnp.float32), pltpu.VMEM((NY - 1,) + shape, jnp.float32),
            dma((NZ - 1,)), dma((NZ - 1,)), dma((NX - 1,)), dma((NX - 1,)),
            dma((NY - 1,)), dma((NY - 1,)), dma, dma,
        ],
        compiler_params=pltpu.CompilerParams(collective_id=1, has_side_effects=True),
        name="stats",
    )(stats)


def gather_kernel(part, out, local_sem, c_send, c_recv, r_send, r_recv):
    x, y, z, c = coords()
    v = vocab_index(x, y, c)
    sibling = (z, vocab_index(x, y, 1 - c))
    devices = (((z + 1) % NZ, v), ((z + NZ - 1) % NZ, v))
    greet([devices[0], devices[1], sibling])
    half = part.shape[0]

    def place(h, block):
        return out.at[
            pl.ds(pl.multiple_of(h * half, 16), half),
            pl.ds(pl.multiple_of(block * ROWS, ROWS), ROWS),
        ]

    def columns(k):
        return part.at[:, pl.ds(pl.multiple_of(k * ROWS, ROWS), ROWS)]

    local = pltpu.make_async_copy(columns(c), place(c, z), local_sem)
    share = remote(columns(1 - c), place(c, z), c_send, c_recv, sibling)
    share.start()
    local.start()

    def ring(step, way, index, arriving):
        h = c if index == 0 else 1 - c
        back = step if arriving else step - 1
        sign = -1 if way == 0 else 1
        block = (z + sign * back + NZ) % NZ
        src = place(h, block)
        if step == 1 and index == 0 and not arriving:
            src = columns(c)
        return remote(
            src, place(h, block), r_send.at[step - 1, way, index],
            r_recv.at[step - 1, way, index], devices[way],
        )

    def ways(step, index):
        return (0, 1) if step < 4 else (index,)

    for way in (0, 1):
        ring(1, way, 0, False).start()
    remote(columns(c), place(1 - c, z), c_send, c_recv, sibling).wait_recv()
    for way in (0, 1):
        ring(1, way, 1, False).start()
    for step in (1, 2, 3):
        for index in (0, 1):
            for way in (0, 1):
                ring(step, way, index, True).wait_recv()
                if way in ways(step + 1, index):
                    ring(step + 1, way, index, False).start()
    for index in (0, 1):
        ring(4, index, index, True).wait_recv()
    local.wait()
    share.wait_send()
    for step in (1, 2, 3, 4):
        for index in (0, 1):
            for way in ways(step, index):
                ring(step, way, index, False).wait_send()


def gather_grads(part):
    anywhere = pl.BlockSpec(memory_space=pl.ANY)
    dma = pltpu.SemaphoreType.DMA
    return pl.pallas_call(
        gather_kernel,
        out_shape=jax.ShapeDtypeStruct((2 * part.shape[0], NZ * ROWS), part.dtype),
        in_specs=[anywhere],
        out_specs=anywhere,
        scratch_shapes=[dma, dma, dma, dma((4, 2, 2)), dma((4, 2, 2))],
        compiler_params=pltpu.CompilerParams(collective_id=2, has_side_effects=True),
        name="gather_grads",
    )(part)


def reduce_kernel(grad, out, cbuf, acc, xbuf, bsum, ybuf, csum, c_send, c_recv,
                  x_send, x_recv, y_send, y_recv, f_send, f_recv, f_local):
    x, y, z, c = coords()
    v = vocab_index(x, y, c)
    sibling = (z, vocab_index(x, y, 1 - c))
    x_peers = [(z, vocab_index((x + s) % NX, y, c)) for s in range(1, NX)]
    y_peers = [(z, vocab_index(x, (y + s) % NY, c)) for s in range(1, NY)]
    dest = (4 * c + y // 2, 8 * z + 2 * x + y % 2)
    j = v % 8
    origin = (v // 8, vocab_index(j // 2, (z % 4) * 2 + j % 2, z // 4))
    stays = jnp.logical_and(dest[0] == z, dest[1] == v)
    leaves = jnp.logical_not(stays)

    barrier = pltpu.get_barrier_semaphore()
    for device in x_peers + y_peers + [sibling]:
        pl.semaphore_signal(barrier, inc=1, device_id=device, device_id_type=MESH)

    @pl.when(leaves)
    def _():
        for device in (dest, origin):
            pl.semaphore_signal(barrier, inc=1, device_id=device, device_id_type=MESH)

    greeted = len(x_peers) + len(y_peers) + 1
    pl.semaphore_wait(barrier, greeted + 2 - 2 * stays.astype(jnp.int32))

    lanes = pl.ds(pl.multiple_of(512 * c, 512), 512)
    other_lanes = pl.ds(pl.multiple_of(512 * (1 - c), 512), 512)

    def rows(q):
        return pl.ds(pl.multiple_of(q * 128, 128), 128)

    order = [(x + s) % NX for s in (2, 1, 3, 0)]
    shares = [
        remote(grad.at[rows(q), other_lanes], cbuf.at[rows(q), :], c_send.at[k], c_recv.at[k], sibling)
        for k, q in enumerate(order)
    ]
    for share in shares:
        share.start()
    x_copies = []
    for k, s in enumerate((2, 1, 3, 0)):
        q = order[k]
        shares[k].wait_recv()
        acc[rows(q), :] = grad[rows(q), lanes] + cbuf[rows(q), :]
        if s:
            copy = remote(
                acc.at[rows(q), :], xbuf.at[s - 1], x_send.at[s - 1], x_recv.at[s - 1],
                x_peers[s - 1],
            )
            copy.start()
            x_copies.append(copy)
    for copy in x_copies:
        copy.wait_recv()
    bsum[...] = acc[rows(x), :] + xbuf[0] + xbuf[1] + xbuf[2]

    def piece(q):
        return (
            pl.ds(pl.multiple_of((q % 2) * 64, 64), 64),
            pl.ds(pl.multiple_of((q // 2) * 128, 128), 128),
        )

    y_copies = []
    for s in FAR_FIRST:
        a, b = piece((y + s) % NY)
        copy = remote(
            bsum.at[a, b], ybuf.at[s - 1], y_send.at[s - 1], y_recv.at[s - 1], y_peers[s - 1]
        )
        copy.start()
        y_copies.append(copy)
    for copy in y_copies:
        copy.wait_recv()
    a, b = piece(y)
    csum[...] = bsum[a, b] + sum(ybuf[s] for s in range(NY - 1))

    final = remote(csum, out, f_send, f_recv, dest)
    stay = pltpu.make_async_copy(csum, out, f_local)

    @pl.when(leaves)
    def _():
        final.start()
        final.wait_recv()
        final.wait_send()

    @pl.when(stays)
    def _():
        stay.start()
        stay.wait()

    for copy in shares + x_copies + y_copies:
        copy.wait_send()


def reduce_grads(grad):
    vmem = pl.BlockSpec(memory_space=pltpu.VMEM)
    dma = pltpu.SemaphoreType.DMA
    f32 = jnp.float32
    return pl.pallas_call(
        reduce_kernel,
        out_shape=jax.ShapeDtypeStruct((64, 128), f32),
        in_specs=[vmem],
        out_specs=vmem,
        scratch_shapes=[
            pltpu.VMEM((512, 512), f32), pltpu.VMEM((512, 512), f32),
            pltpu.VMEM((NX - 1, 128, 512), f32), pltpu.VMEM((128, 512), f32),
            pltpu.VMEM((NY - 1, 64, 128), f32), pltpu.VMEM((64, 128), f32),
            dma((4,)), dma((4,)), dma((NX - 1,)), dma((NX - 1,)),
            dma((NY - 1,)), dma((NY - 1,)), dma, dma, dma,
        ],
        compiler_params=pltpu.CompilerParams(
            collective_id=3, has_side_effects=True, vmem_limit_bytes=24 * 1024 * 1024
        ),
        name="reduce_grads",
    )(grad)


def body(hidden_ref, hidden_train, head_ref, head_train, targets, mask):
    f32 = jnp.float32
    vocab_rows = head_train.shape[0]
    x, y, z, c = coords()
    chip = lax.axis_index("vocab") // 2
    contract_last = (((1,), (1,)), ((), ()))

    meta = jnp.zeros((8, 256), jnp.int32)
    meta = meta.at[0, :TOK].set(targets).at[1, :TOK].set(mask)
    x_ref, x_train, g_ref, g_train, meta_all = spread(
        hidden_ref, hidden_train, head_ref, head_train, meta
    )
    targets_all = meta_all[:, 0, :TOK]
    mask_all = meta_all[:, 1, :TOK]
    half_targets = lax.dynamic_slice_in_dim(targets_all, 4 * c, 4, 0).reshape(4 * TOK)
    half_mask = lax.dynamic_slice_in_dim(mask_all, 4 * c, 4, 0)

    train_logits = lax.dot_general(x_train, g_train, contract_last, preferred_element_type=f32)
    ref_logits = lax.dot_general(x_ref, g_ref, contract_last, preferred_element_type=f32)

    column = jnp.arange(2 * ROWS, dtype=jnp.int32)
    start = z * ROWS - 16 * (z // 7)
    row_id = (2 * chip + column // ROWS) * vocab_rows + start + column % ROWS
    valid = jnp.logical_or(z < 7, column % ROWS >= 16)
    hit = jnp.logical_and(row_id[None, :] == half_targets[:, None], valid[None, :])

    def local_stats(logits):
        top = jnp.max(jnp.where(valid[None, :], logits, -jnp.inf), axis=1)
        total = jnp.sum(jnp.where(valid[None, :], jnp.exp(logits - top[:, None]), 0.0), axis=1)
        picked = jnp.sum(jnp.where(hit, logits, 0.0), axis=1)
        return [top, total, picked]

    zeros = jnp.zeros((4 * TOK,), f32)
    stats = jnp.stack(local_stats(ref_logits) + local_stats(train_logits) + [zeros, zeros])
    both = exchange_stats(stats)

    ce_ref = jnp.log(both[:, 1]) + both[:, 0] - both[:, 2]
    ce_train = jnp.log(both[:, 4]) + both[:, 3] - both[:, 5]
    excess_all = (ce_train - ce_ref).reshape(NZ, TOK)
    excess = lax.dynamic_slice_in_dim(excess_all, z, 1, 0).reshape(TOK)
    weight_all = mask_all.astype(f32)
    loss_value = jnp.sum(weight_all * ce_train.reshape(NZ, TOK)) / (NZ * SEL)

    own = lax.dynamic_slice_in_dim(both, c, 1, 0)[0]
    probabilities = jnp.exp(train_logits - own[3][:, None]) / own[4][:, None]
    logit_grads = jnp.where(
        valid[None, :], loss_scale * (probabilities - hit.astype(f32)), 0.0
    ).astype(jnp.bfloat16)

    rank = jnp.cumsum(half_mask, axis=1) - 1
    pick = jnp.logical_and(
        rank[:, None, :] == jnp.arange(SLOT, dtype=jnp.int32)[None, :, None],
        half_mask[:, None, :] != 0,
    ).astype(jnp.bfloat16)
    chosen = lax.dot_general(
        pick, logit_grads.reshape(4, TOK, 2 * ROWS), (((2,), (1,)), ((0,), (0,))),
        preferred_element_type=f32,
    ).astype(jnp.bfloat16).reshape(4 * SLOT, 2 * ROWS)

    grads = gather_grads(chosen)
    slotted = jnp.pad(grads.reshape(NZ, SLOT, NZ * ROWS), ((0, 0), (0, 128 - SLOT), (0, 0)))
    slotted = slotted.reshape(NZ * 128, NZ * ROWS)
    home = jnp.concatenate([head_train[:7 * ROWS], head_train[7 * ROWS - 16:]], axis=0)
    partial_grad = lax.dot_general(
        home, slotted, (((0,), (1,)), ((), ())), preferred_element_type=f32
    )
    piece = reduce_grads(partial_grad)

    own_rank = jnp.cumsum(mask) - 1
    place = jnp.logical_and(
        jnp.arange(128, dtype=jnp.int32)[:, None] == own_rank[None, :], mask[None, :] != 0
    ).astype(f32)
    hidden_grad = lax.dot_general(
        piece, place, (((1,), (0,)), ((), ())), precision=lax.Precision.HIGHEST,
        preferred_element_type=f32,
    )
    return (excess, loss_value, hidden_grad)


def solution(mesh):
    in_specs = (P("dp", None), P("dp", None), P("vocab", "dp"), P("vocab", "dp"), P("dp"), P("dp"))
    out_specs = (P("dp"), P(), P("vocab", "dp"))
    return jax.shard_map(body, mesh=mesh, in_specs=in_specs, out_specs=out_specs, check_vma=False)
```

```python
import functools

import jax
import jax.numpy as jnp
from jax import lax
from jax.experimental import pallas as pl
from jax.experimental.pallas import tpu as pltpu
from jax.sharding import PartitionSpec as P

MESH = pl.DeviceIdType.MESH
NX, NY, NZ = 4, 8, 8
loss_scale = 64.0
TOK = 160
SEL = 100
SLOT = 112
ROWS = 128
PIECE = 128
FEAT = 512
WIDTH = 4096
HALF = 4 * SLOT
LANES = 256
FAR_FIRST = (4, 3, 5, 2, 6, 1, 7)
NEAR_FIRST = (1, 7, 2, 6, 3, 5, 4)
LAST = (((1,), (1,)), ((), ()))
REF, TRAIN = 0, 1


def coords():
    z = lax.axis_index("dp")
    v = lax.axis_index("vocab")
    return v // 16, (v // 2) % NY, z, v % 2


def vocab_index(x, y, c):
    return (x * NY + y) * 2 + c


def remote(src, dst, send_sem, recv_sem, device):
    return pltpu.make_async_remote_copy(
        src_ref=src, dst_ref=dst, send_sem=send_sem, recv_sem=recv_sem,
        device_id=device, device_id_type=MESH,
    )


def aligned(start, size, step):
    return pl.ds(pl.multiple_of(start, step), size)


def kernel(
    hid_ref, hid_train, head_ref, head_train, meta,
    piece_out, stats_out, meta_all,
    xbuf, gbuf, home, logits, stats, zstat, xstat, ystat,
    chosen, gathered, grad, cgrad, acc, xgrad, turned, ygrad, summed,
    local_sem, z_send, z_recv, m_send, m_recv, w_send, w_recv, s_send, s_recv,
    rx_send, rx_recv, ry_send, ry_recv,
    tz_send, tz_recv, tx_send, tx_recv, ty_send, ty_recv, tc_send, tc_recv,
    ec_send, ec_recv, ez_send, ez_recv,
    gc_send, gc_recv, gx_send, gx_recv, gy_send, gy_recv, f_send, f_recv,
):
    f32 = jnp.float32
    x, y, z, c = coords()
    v = vocab_index(x, y, c)
    sibling = (z, vocab_index(x, y, 1 - c))
    z_peers = [None] + [((z + s) % NZ, v) for s in range(1, NZ)]
    x_peers = [None] + [(z, vocab_index((x + s) % NX, y, c)) for s in range(1, NX)]
    y_peers = [None] + [(z, vocab_index(x, (y + s) % NY, c)) for s in range(1, NY)]
    dest = (4 * c + y // 2, 8 * z + 2 * x + y % 2)
    j = v % 8
    origin = (v // 8, vocab_index(j // 2, (z % 4) * 2 + j % 2, z // 4))
    stays = jnp.logical_and(dest[0] == z, dest[1] == v)
    leaves = jnp.logical_not(stays)

    barrier = pltpu.get_barrier_semaphore()
    friends = z_peers[1:] + x_peers[1:] + y_peers[1:] + [sibling]
    for device in friends:
        pl.semaphore_signal(barrier, inc=1, device_id=device, device_id_type=MESH)

    @pl.when(leaves)
    def _():
        for device in (dest, origin):
            pl.semaphore_signal(barrier, inc=1, device_id=device, device_id_type=MESH)

    pl.semaphore_wait(barrier, len(friends) + 2 - 2 * stays.astype(jnp.int32))

    is_source = z // 4 == c
    hid = (hid_ref, hid_train)
    heads = (head_ref, head_train)

    def when_active(r, act):
        if r:
            act()
        else:
            pl.when(jnp.logical_not(is_source))(act)

    def own_piece(r):
        if r < 2:
            return aligned((y * NX + x) * PIECE, PIECE, PIECE)
        return aligned((x * NY + y) * PIECE, PIECE, PIECE)

    def z_copy(a, s):
        columns = own_piece(-s % 4)
        return remote(
            hid[a].at[:, columns], xbuf.at[a, aligned(TOK * (z % 4), TOK, 16), columns],
            z_send.at[a, s - 1], z_recv.at[a, -s % 4], z_peers[s],
        )

    def z_arrival(a, r):
        columns = own_piece(r)
        part = xbuf.at[a, aligned(TOK * ((z + r) % 4), TOK, 16), columns]
        return remote(part, part, z_send.at[a, 0], z_recv.at[a, r], sibling)

    def own_tokens(a):
        return pltpu.make_async_copy(
            hid[a], xbuf.at[a, aligned(TOK * (z % 4), TOK, 16), :], local_sem.at[a]
        )

    def meta_copy(s, arriving):
        source = (z + NZ - s) % NZ if arriving else z
        return remote(meta, meta_all.at[source], m_send.at[s - 1], m_recv.at[s - 1], z_peers[s])

    def row_block(q):
        return aligned(q * ROWS - 16 * (q // 7), ROWS, 16)

    def head_part(a, core, source):
        return gbuf.at[a, aligned(ROWS * core, ROWS, ROWS), aligned(source * FEAT, FEAT, FEAT)]

    def head_copy(a, s, arriving):
        source = (z + NZ - s) % NZ if arriving else z
        return remote(
            heads[a].at[row_block((z + s) % NZ), :], head_part(a, c, source),
            w_send.at[a, s - 1], w_recv.at[a, s - 1], z_peers[s],
        )

    def own_rows(a):
        return pltpu.make_async_copy(
            heads[a].at[row_block(z), :], head_part(a, c, z), local_sem.at[2 + a]
        )

    def share_copy(a, s, arriving):
        part = head_part(a, 1 - c if arriving else c, (z + NZ - s) % NZ)
        return remote(part, part, s_send.at[a, s], s_recv.at[a, s], sibling)

    own_meta = pltpu.make_async_copy(meta, meta_all.at[z], local_sem.at[4])
    home_copies = [
        pltpu.make_async_copy(
            head_train.at[pl.ds(0, 7 * ROWS), :], home.at[pl.ds(0, 7 * ROWS), :], local_sem.at[5]
        ),
        pltpu.make_async_copy(
            head_train.at[pl.ds(7 * ROWS - 16, ROWS), :], home.at[pl.ds(7 * ROWS, ROWS), :],
            local_sem.at[6],
        ),
    ]

    def ring_copy(a, r, axis, step, way, arriving):
        size, pos, peers = (NX, x, x_peers) if axis == "x" else (NY, y, y_peers)
        send, recv = (rx_send, rx_recv) if axis == "x" else (ry_send, ry_recv)
        back = step if arriving else step - 1
        sign = -1 if way == 0 else 1
        block = (pos + sign * back + size) % size
        group = NX * PIECE if r < 2 else NY * PIECE
        if (axis == "x") == (r < 2):
            base = y if r < 2 else x
            columns = aligned(base * group + block * PIECE, PIECE, PIECE)
        else:
            columns = aligned(block * group, group, group)
        start = TOK * ((z + r) % 4)
        if 2 * step == size:
            rows = aligned(start + way * (TOK // 2), TOK // 2, 16)
        else:
            rows = aligned(start, TOK, 16)
        part = xbuf.at[a, rows, columns]
        index = (a, r, step - 1, way)
        return remote(part, part, send.at[index], recv.at[index], peers[1 if way == 0 else size - 1])

    def ring_send(a, r, axis, step):
        for way in (0, 1):
            ring_copy(a, r, axis, step, way, False).start()

    def ring_wait(a, r, axis, step):
        for way in (0, 1):
            ring_copy(a, r, axis, step, way, True).wait_recv()

    def advance(a, *moves):
        for group, axis, step, next_axis, next_step in moves:
            for r in group:
                def act(r=r):
                    ring_wait(a, r, axis, step)
                    if next_axis:
                        ring_send(a, r, next_axis, next_step)
                when_active(r, act)

    A, B = (1, 0), (2, 3)

    def start_rings(a):
        for r in (2, 3, 1, 0):
            def act(r=r):
                z_arrival(a, r).wait_recv()
                ring_send(a, r, "x" if r < 2 else "y", 1)
            when_active(r, act)

    def pass_heads(a, distances):
        for s in distances:
            head_copy(a, s, True).wait_recv()
            share_copy(a, s, False).start()

    for a in (TRAIN, REF):
        @pl.when(is_source)
        def _():
            for s in FAR_FIRST:
                z_copy(a, s).start()
            own_tokens(a).start()
        if a == TRAIN:
            own_meta.start()
            for s in range(1, NZ):
                meta_copy(s, False).start()
        own_rows(a).start()
        for s in FAR_FIRST:
            head_copy(a, s, False).start()
    for copy in home_copies:
        copy.start()
    zero_stats = jnp.zeros((16, LANES), f32)
    for a in (REF, TRAIN):
        stats[a, 0] = zero_stats

    start_rings(TRAIN)
    advance(TRAIN, (B, "y", 1, "y", 2), (A, "x", 1, "x", 2))
    advance(TRAIN, (B, "y", 2, "y", 3), (A, "x", 2, "y", 1))
    advance(TRAIN, (B, "y", 3, "y", 4))
    advance(TRAIN, (B, "y", 4, "x", 1))
    own_rows(TRAIN).wait()
    share_copy(TRAIN, 0, False).start()
    advance(TRAIN, (A, "y", 1, "y", 2))
    start_rings(REF)
    advance(TRAIN, (A, "y", 2, "y", 3))
    pass_heads(TRAIN, (1, 7, 2, 6))
    advance(TRAIN, (B, "x", 1, "x", 2))
    advance(REF, (B, "y", 1, "y", 2), (A, "x", 1, "x", 2))
    advance(TRAIN, (A, "y", 3, "y", 4))
    advance(REF, (B, "y", 2, "y", 3), (A, "x", 2, "y", 1))
    pass_heads(TRAIN, (3, 5, 4))
    advance(REF, (B, "y", 3, "y", 4))
    advance(REF, (B, "y", 4, "x", 1))
    advance(TRAIN, (A, "y", 4, None, 0), (B, "x", 2, None, 0))
    own_meta.wait()
    for s in range(1, NZ):
        meta_copy(s, True).wait_recv()
    for s in range(NZ):
        share_copy(TRAIN, s, True).wait_recv()

    @pl.when(is_source)
    def _():
        own_tokens(TRAIN).wait()

    row = lax.broadcasted_iota(jnp.int32, (2 * ROWS, TOK), 0)
    within = row % ROWS
    chip = v // 2
    row_id = (2 * chip + row // ROWS) * 1008 + z * ROWS - 16 * (z // 7) + within
    valid = jnp.logical_or(within >= 16, z < 7)

    def hits(i):
        return jnp.logical_and(row_id == meta_all[4 * c + i][0:1, :TOK], valid)

    def local_stats(a):
        for i in range(4):
            table = lax.dot_general(
                gbuf[a], xbuf[a, TOK * i:TOK * (i + 1), :], LAST, preferred_element_type=f32
            )
            if a == TRAIN:
                logits[i] = table
            top = jnp.max(jnp.where(valid, table, -jnp.inf), axis=0, keepdims=True)
            parts = jnp.where(valid, jnp.exp(table - top), 0.0)
            picked = jnp.where(hits(i), table, 0.0)
            stats[a, 0, i:i + 1, :TOK] = top
            stats[a, 0, 4 + i:5 + i, :TOK] = jnp.sum(parts, axis=0, keepdims=True)
            stats[a, 0, 8 + i:9 + i, :TOK] = jnp.sum(picked, axis=0, keepdims=True)

    levels = (
        (z_peers, zstat, tz_send, tz_recv),
        (x_peers, xstat, tx_send, tx_recv),
        (y_peers, ystat, ty_send, ty_recv),
    )

    def stat_copies(a, level):
        peers, buf, send, recv = levels[level]
        return [
            remote(stats.at[a, level], buf.at[a, s], send.at[a, s], recv.at[a, s], peers[s + 1])
            for s in range(len(peers) - 1)
        ]

    def stat_send(a, level):
        for copy in stat_copies(a, level):
            copy.start()

    def stat_merge(a, level):
        copies = stat_copies(a, level)
        for copy in copies:
            copy.wait_recv()
        blocks = [stats[a, level]] + [levels[level][1][a, s] for s in range(len(copies))]
        top = functools.reduce(jnp.maximum, [b[0:4] for b in blocks])
        total = sum(b[4:8] * jnp.exp(b[0:4] - top) for b in blocks)
        picked = sum(b[8:12] for b in blocks)
        merged = jnp.concatenate([top, total, picked, jnp.zeros_like(top)], axis=0)
        if level < 2:
            stats[a, level + 1] = merged
        else:
            stats_out[a, c] = merged

    def stat_share(a, arriving):
        part = stats_out.at[a, 1 - c if arriving else c]
        return remote(part, part, tc_send.at[a], tc_recv.at[a], sibling)

    local_stats(TRAIN)
    stat_send(TRAIN, 0)
    advance(REF, (A, "y", 1, "y", 2))
    stat_merge(TRAIN, 0)
    stat_send(TRAIN, 1)
    advance(REF, (A, "y", 2, "y", 3))
    stat_merge(TRAIN, 1)
    stat_send(TRAIN, 2)
    own_rows(REF).wait()
    share_copy(REF, 0, False).start()
    stat_merge(TRAIN, 2)
    stat_share(TRAIN, False).start()

    upper = (
        lax.broadcasted_iota(jnp.int32, (TOK, TOK), 0)
        <= lax.broadcasted_iota(jnp.int32, (TOK, TOK), 1)
    ).astype(jnp.bfloat16)
    place = lax.broadcasted_iota(jnp.int32, (SLOT, TOK), 0)
    for i in range(4):
        weight = meta_all[4 * c + i][1:2, :TOK]
        count = jnp.dot(
            jnp.broadcast_to(weight, (8, TOK)).astype(jnp.bfloat16), upper,
            preferred_element_type=f32,
        )[0:1].astype(jnp.int32)
        pick = jnp.logical_and(place == count - 1, weight != 0).astype(jnp.bfloat16)
        top = stats_out[TRAIN, c][i:i + 1, :TOK]
        total = stats_out[TRAIN, c][4 + i:5 + i, :TOK]
        share = jnp.exp(logits[i] - top) / total
        slope = jnp.where(valid, loss_scale * (share - hits(i).astype(f32)), 0.0)
        rows = lax.dot_general(
            pick, slope.astype(jnp.bfloat16), LAST, preferred_element_type=f32
        ).astype(jnp.bfloat16)
        for k in (0, 1):
            chosen[k, SLOT * i:SLOT * (i + 1), :] = rows[:, ROWS * k:ROWS * (k + 1)]

    def half_rows(h):
        return aligned(h * HALF, HALF, 16)

    own_chosen = pltpu.make_async_copy(
        chosen.at[c], gathered.at[z, half_rows(c), :], local_sem.at[7]
    )
    chosen_share = remote(
        chosen.at[1 - c], gathered.at[z, half_rows(c), :], ec_send, ec_recv, sibling
    )
    chosen_arrival = remote(
        chosen.at[c], gathered.at[z, half_rows(1 - c), :], ec_send, ec_recv, sibling
    )

    def e_copy(step, way, index, arriving):
        h = c if index == 0 else 1 - c
        back = step if arriving else step - 1
        sign = -1 if way == 0 else 1
        part = gathered.at[(z + sign * back + NZ) % NZ, half_rows(h), :]
        src = chosen.at[c] if step == 1 and index == 0 and not arriving else part
        return remote(
            src, part, ez_send.at[step - 1, way, index], ez_recv.at[step - 1, way, index],
            z_peers[1 if way == 0 else NZ - 1],
        )

    def e_advance(step):
        for index in (0, 1):
            for way in (0, 1):
                if step < 4 or way == index:
                    e_copy(step, way, index, True).wait_recv()
                if step < 3 or (step == 3 and way == index):
                    e_copy(step + 1, way, index, False).start()

    chosen_share.start()
    for way in (0, 1):
        e_copy(1, way, 0, False).start()
    own_chosen.start()
    chosen_arrival.wait_recv()
    for way in (0, 1):
        e_copy(1, way, 1, False).start()
    advance(REF, (A, "y", 3, "y", 4), (B, "x", 1, "x", 2))
    e_advance(1)
    pass_heads(REF, (1, 7))
    e_advance(2)
    pass_heads(REF, (2, 6))
    e_advance(3)
    pass_heads(REF, (3, 5, 4))
    advance(REF, (A, "y", 4, None, 0), (B, "x", 2, None, 0))
    for s in range(NZ):
        share_copy(REF, s, True).wait_recv()

    @pl.when(is_source)
    def _():
        own_tokens(REF).wait()

    local_stats(REF)
    stat_send(REF, 0)
    e_advance(4)
    own_chosen.wait()
    for copy in home_copies:
        copy.wait()

    for d in range(NZ):
        columns = jnp.concatenate(
            [gathered[q, SLOT * d:SLOT * (d + 1), :] for q in range(NZ)], axis=1
        )
        table = jnp.dot(columns, home[...], preferred_element_type=f32)
        for q in range(NX):
            grad[q, SLOT * d:SLOT * (d + 1), :] = table[:, 128 * q:128 * (q + 1)]

    def grad_share(q):
        return remote(
            grad.at[q, aligned(HALF * (1 - c), HALF, 16), :], cgrad.at[q],
            gc_send.at[q], gc_recv.at[q], sibling,
        )

    def x_copy(s):
        return remote(
            acc.at[(x + s) % NX], xgrad.at[s - 1], gx_send.at[s - 1], gx_recv.at[s - 1], x_peers[s]
        )

    def y_copy(s):
        q = (y + s) % NY
        return remote(
            turned.at[q // 2, aligned((q % 2) * 64, 64, 64), :], ygrad.at[s - 1],
            gy_send.at[s - 1], gy_recv.at[s - 1], y_peers[s],
        )

    order = (2, 1, 3, 0)
    for s in order:
        grad_share((x + s) % NX).start()
    for s in order:
        q = (x + s) % NX
        grad_share(q).wait_recv()
        acc[q] = grad[q, aligned(HALF * c, HALF, 16), :] + cgrad[q]
        if s:
            x_copy(s).start()
    stat_merge(REF, 0)
    stat_send(REF, 1)
    for s in range(1, NX):
        x_copy(s).wait_recv()
    total = acc[x] + xgrad[0] + xgrad[1] + xgrad[2]
    for i in range(4):
        block = jnp.concatenate(
            [total[SLOT * i:SLOT * (i + 1)], jnp.zeros((128 - SLOT, 128), f32)], axis=0
        )
        turned[i] = block.T
    for s in FAR_FIRST:
        y_copy(s).start()
    stat_merge(REF, 1)
    stat_send(REF, 2)
    for s in range(1, NY):
        y_copy(s).wait_recv()
    summed[...] = turned[y // 2, aligned((y % 2) * 64, 64, 64), :] + sum(
        ygrad[s] for s in range(NY - 1)
    )
    final = remote(summed, piece_out, f_send, f_recv, dest)
    stay = pltpu.make_async_copy(summed, piece_out, local_sem.at[8])

    @pl.when(leaves)
    def _():
        final.start()

    @pl.when(stays)
    def _():
        stay.start()

    stat_merge(REF, 2)
    stat_share(REF, False).start()
    for a in (TRAIN, REF):
        stat_share(a, True).wait_recv()

    @pl.when(leaves)
    def _():
        final.wait_recv()
        final.wait_send()

    @pl.when(stays)
    def _():
        stay.wait()

    for a in (REF, TRAIN):
        @pl.when(is_source)
        def _():
            for s in range(1, NZ):
                z_copy(a, s).wait_send()
        for s in range(1, NZ):
            head_copy(a, s, False).wait_send()
        for s in range(NZ):
            share_copy(a, s, False).wait_send()
        for level in range(3):
            for copy in stat_copies(a, level):
                copy.wait_send()
        stat_share(a, False).wait_send()
        for r in range(4):
            def act(r=r):
                for axis, size in (("x", NX), ("y", NY)):
                    for step in range(1, size // 2 + 1):
                        for way in (0, 1):
                            ring_copy(a, r, axis, step, way, False).wait_send()
            when_active(r, act)
    for s in range(1, NZ):
        meta_copy(s, False).wait_send()
    chosen_share.wait_send()
    for step in (1, 2, 3, 4):
        for index in (0, 1):
            for way in (0, 1):
                if step < 4 or way == index:
                    e_copy(step, way, index, False).wait_send()
    for q in range(NX):
        grad_share(q).wait_send()
    for s in range(1, NX):
        x_copy(s).wait_send()
    for s in range(1, NY):
        y_copy(s).wait_send()


def fused(hidden_ref, hidden_train, head_ref, head_train, meta):
    anywhere = pl.BlockSpec(memory_space=pl.ANY)
    vmem = pl.BlockSpec(memory_space=pltpu.VMEM)
    dma = pltpu.SemaphoreType.DMA
    sds = jax.ShapeDtypeStruct
    f32, bf16 = jnp.float32, jnp.bfloat16
    buf = pltpu.VMEM
    pairs = [
        (2, NZ - 1), (2, 4), (NZ - 1,), (NZ - 1,), (2, NZ - 1), (2, NZ - 1), (2, NZ), (2, NZ),
        (2, 4, 2, 2), (2, 4, 2, 2), (2, 4, 4, 2), (2, 4, 4, 2),
        (2, NZ - 1), (2, NZ - 1), (2, NX - 1), (2, NX - 1), (2, NY - 1), (2, NY - 1), (2,), (2,),
    ]
    return pl.pallas_call(
        kernel,
        out_shape=[
            sds((64, 128), f32), sds((2, 2, 16, LANES), f32), sds((NZ,) + meta.shape, meta.dtype),
        ],
        in_specs=[anywhere] * 5,
        out_specs=[vmem] * 3,
        scratch_shapes=[
            buf((2, 4 * TOK, WIDTH), bf16), buf((2, 2 * ROWS, WIDTH), bf16),
            buf((NZ * ROWS, FEAT), bf16), buf((4, 2 * ROWS, TOK), f32),
            buf((2, 3, 16, LANES), f32), buf((2, NZ - 1, 16, LANES), f32),
            buf((2, NX - 1, 16, LANES), f32), buf((2, NY - 1, 16, LANES), f32),
            buf((2, HALF, ROWS), bf16), buf((NZ, 2 * HALF, ROWS), bf16),
            buf((NX, 2 * HALF, 128), f32), buf((NX, HALF, 128), f32), buf((NX, HALF, 128), f32),
            buf((NX - 1, HALF, 128), f32), buf((4, 128, 128), f32),
            buf((NY - 1, 64, 128), f32), buf((64, 128), f32),
            dma((9,)), *[dma(shape) for shape in pairs],
            dma, dma, dma((4, 2, 2)), dma((4, 2, 2)),
            dma((NX,)), dma((NX,)), dma((NX - 1,)), dma((NX - 1,)),
            dma((NY - 1,)), dma((NY - 1,)), dma, dma,
        ],
        compiler_params=pltpu.CompilerParams(
            collective_id=0, has_side_effects=True, vmem_limit_bytes=60 * 1024 * 1024
        ),
        name="fused",
    )(hidden_ref, hidden_train, head_ref, head_train, meta)


def body(hidden_ref, hidden_train, head_ref, head_train, targets, mask):
    f32 = jnp.float32
    x, y, z, c = coords()
    meta = jnp.pad(jnp.stack([targets, mask]), ((0, 6), (0, LANES - TOK)))
    piece, both, meta_all = fused(hidden_ref, hidden_train, head_ref, head_train, meta)

    both = both[:, :, :12, :TOK].reshape(2, 2, 3, 4, TOK)
    cross = jnp.log(both[:, :, 1]) + both[:, :, 0] - both[:, :, 2]
    cross = cross.reshape(2, NZ, TOK)
    excess_all = cross[TRAIN] - cross[REF]
    excess = lax.dynamic_slice_in_dim(excess_all, z, 1, 0).reshape(TOK)
    weight_all = meta_all[:, 1, :TOK].astype(f32)
    loss_value = jnp.sum(weight_all * cross[TRAIN]) / (NZ * SEL)

    upper = jnp.triu(jnp.ones((TOK, TOK), f32))
    count = jnp.dot(mask.astype(f32)[None, :], upper)
    place = jnp.logical_and(
        jnp.arange(128, dtype=f32)[:, None] == count - 1.0, mask[None, :] != 0
    ).astype(f32)
    hidden_grad = lax.dot_general(
        piece, place, (((1,), (0,)), ((), ())), precision=lax.Precision.HIGHEST,
        preferred_element_type=f32,
    )
    return (excess, loss_value, hidden_grad)


def solution(mesh):
    in_specs = (P("dp", None), P("dp", None), P("vocab", "dp"), P("vocab", "dp"), P("dp"), P("dp"))
    out_specs = (P("dp"), P(), P("vocab", "dp"))
    return jax.shard_map(body, mesh=mesh, in_specs=in_specs, out_specs=out_specs, check_vma=False)
```

```python
import functools

import jax
import jax.numpy as jnp
from jax import lax
from jax.experimental import pallas as pl
from jax.experimental.pallas import tpu as pltpu
from jax.sharding import PartitionSpec as P

MESH = pl.DeviceIdType.MESH
NX, NY, NZ = 4, 8, 8
loss_scale = 64.0
TOK = 160
SEL = 100
SLOT = 112
ROWS = 128
PIECE = 128
FEAT = 512
WIDTH = 4096
PAIR = 2 * SLOT
LANES = 256
BOTH = 2 * ROWS
FAR_FIRST = (4, 3, 5, 2, 6, 1, 7)
LAST = (((1,), (1,)), ((), ()))
REF, TRAIN = 0, 1


def coords():
    z = lax.axis_index("dp")
    v = lax.axis_index("vocab")
    return v // 16, (v // 2) % NY, z, v % 2


def vocab_index(x, y, c):
    return (x * NY + y) * 2 + c


def remote(src, dst, send_sem, recv_sem, device):
    return pltpu.make_async_remote_copy(
        src_ref=src, dst_ref=dst, send_sem=send_sem, recv_sem=recv_sem,
        device_id=device, device_id_type=MESH,
    )


def aligned(start, size, step):
    return pl.ds(pl.multiple_of(start, step), size)


def kernel(
    hid_ref, hid_train, head_ref, head_train, meta,
    grad_out, excess_out, loss_out,
    meta_all, both, xbuf, gbuf, home, logits, stats, zstat, xstat, ystat,
    gathered, grad, xgrad, turned, ygrad, summed, piece,
    local_sem, z_send, z_recv, m_send, m_recv, w_send, w_recv, s_send, s_recv,
    h_local, h_send, h_recv, ay_send, ay_recv, by_send, by_recv, bx_send, bx_recv,
    tz_send, tz_recv, tx_send, tx_recv, ty_send, ty_recv, tc_send, tc_recv,
    ez_send, ez_recv, gx_send, gx_recv, gy_send, gy_recv, f_send, f_recv,
):
    f32 = jnp.float32
    x, y, z, c = coords()
    v = vocab_index(x, y, c)
    sibling = (z, vocab_index(x, y, 1 - c))
    z_peers = [None] + [((z + s) % NZ, v) for s in range(1, NZ)]
    x_peers = [None] + [(z, vocab_index((x + s) % NX, y, c)) for s in range(1, NX)]
    y_peers = [None] + [(z, vocab_index(x, (y + s) % NY, c)) for s in range(1, NY)]
    dests = [(4 * c + 2 * b + y // 4, 8 * z + 2 * x + (y % 4) // 2) for b in (0, 1)]
    origins = [
        (v // 8, vocab_index((v % 8) // 2, 4 * (z % 2) + 2 * (v % 2) + h, z // 4)) for h in (0, 1)
    ]

    def is_here(device):
        return jnp.logical_and(device[0] == z, device[1] == v)

    barrier = pltpu.get_barrier_semaphore()
    friends = z_peers[1:] + x_peers[1:] + y_peers[1:] + [sibling]
    for device in friends:
        pl.semaphore_signal(barrier, inc=1, device_id=device, device_id_type=MESH)
    expected = len(friends) + 4
    for device in dests + origins:
        expected = expected - is_here(device).astype(jnp.int32)

        @pl.when(jnp.logical_not(is_here(device)))
        def _():
            pl.semaphore_signal(barrier, inc=1, device_id=device, device_id_type=MESH)

    pl.semaphore_wait(barrier, expected)

    is_source = z // 4 == c
    hid = (hid_ref, hid_train)
    heads = (head_ref, head_train)

    def when_active(r, act):
        if r:
            act()
        else:
            pl.when(jnp.logical_not(is_source))(act)

    def z_columns(r):
        if r < 2:
            return aligned(y * FEAT, FEAT, FEAT)
        return aligned((x * NY + y) * PIECE, PIECE, PIECE)

    def z_copy(a, s):
        r = -s % 4
        columns = z_columns(r)
        return remote(
            hid[a].at[:, columns], xbuf.at[a, pl.ds(TOK * r, TOK), columns],
            z_send.at[a, s - 1], z_recv.at[a, r], z_peers[s],
        )

    def z_arrival(a, r):
        part = xbuf.at[a, pl.ds(TOK * r, TOK), z_columns(r)]
        return remote(part, part, z_send.at[a, 0], z_recv.at[a, r], sibling)

    def own_tokens(a):
        return pltpu.make_async_copy(hid[a], xbuf.at[a, pl.ds(0, TOK), :], local_sem.at[a])

    def meta_copy(s, arriving):
        source = (z + NZ - s) % NZ if arriving else z
        return remote(meta, meta_all.at[source], m_send.at[s - 1], m_recv.at[s - 1], z_peers[s])

    def row_block(q):
        return aligned(q * ROWS - 16 * (q // 7), ROWS, 16)

    def head_part(a, core, source):
        return gbuf.at[a, aligned(ROWS * core, ROWS, ROWS), aligned(source * FEAT, FEAT, FEAT)]

    def head_copy(a, s, arriving):
        source = (z + NZ - s) % NZ if arriving else z
        return remote(
            heads[a].at[row_block((z + s) % NZ), :], head_part(a, c, source),
            w_send.at[a, s - 1], w_recv.at[a, s - 1], z_peers[s],
        )

    def own_rows(a):
        return pltpu.make_async_copy(
            heads[a].at[row_block(z), :], head_part(a, c, z), local_sem.at[2 + a]
        )

    def share_copy(a, s, arriving):
        part = head_part(a, 1 - c if arriving else c, (z + NZ - s) % NZ)
        return remote(part, part, s_send.at[a, s], s_recv.at[a, s], sibling)

    own_meta = pltpu.make_async_copy(meta, meta_all.at[z], local_sem.at[4])

    def home_local(q):
        return pltpu.make_async_copy(
            head_train.at[row_block(q), :], home.at[aligned(q * BOTH + c * ROWS, ROWS, ROWS), :],
            h_local.at[q],
        )

    def home_copy(q, arriving):
        core = 1 - c if arriving else c
        return remote(
            head_train.at[row_block(q), :], home.at[aligned(q * BOTH + core * ROWS, ROWS, ROWS), :],
            h_send.at[q], h_recv.at[q], sibling,
        )

    def around(peers, way):
        return peers[1 if way == 0 else len(peers) - 1]

    def back_of(step, way, arriving):
        back = step if arriving else step - 1
        return -back if way == 0 else back

    def a_copy(a, r, step, way, arriving):
        block = (y + back_of(step, way, arriving) + NY) % NY
        rows = pl.ds(TOK * r, TOK) if step < 4 else pl.ds(TOK * r + 80 * way, 80)
        part = xbuf.at[a, rows, aligned(block * FEAT, FEAT, FEAT)]
        index = (a, r, step - 1, way)
        return remote(part, part, ay_send.at[index], ay_recv.at[index], around(y_peers, way))

    def b_rows(step, last, way):
        return pl.ds(2 * TOK, 2 * TOK) if step < last else pl.ds(2 * TOK + TOK * way, TOK)

    def by_copy(a, step, way, arriving):
        block = x * NY + (y + back_of(step, way, arriving) + NY) % NY
        part = xbuf.at[a, b_rows(step, 4, way), aligned(block * PIECE, PIECE, PIECE)]
        index = (a, step - 1, way)
        return remote(part, part, by_send.at[index], by_recv.at[index], around(y_peers, way))

    def bx_copy(a, far, step, way, arriving):
        block = ((x + back_of(step, way, arriving) + NX) % NX) * NY + (y + far) % NY
        part = xbuf.at[a, b_rows(step, 2, way), aligned(block * PIECE, PIECE, PIECE)]
        index = (a, far, step - 1, way)
        return remote(part, part, bx_send.at[index], bx_recv.at[index], around(x_peers, way))

    def a_move(a, step):
        for r in (1, 0):
            def act(r=r):
                for way in (0, 1):
                    a_copy(a, r, step, way, True).wait_recv()
                    if step < 4:
                        a_copy(a, r, step + 1, way, False).start()
            when_active(r, act)

    def bx_start(a, *fars):
        for far in fars:
            for way in (0, 1):
                bx_copy(a, far % NY, 1, way, False).start()

    def bx_move(a, step, *fars):
        for far in fars:
            for way in (0, 1):
                bx_copy(a, far % NY, step, way, True).wait_recv()
                if step == 1:
                    bx_copy(a, far % NY, 2, way, False).start()

    def by_move(a, step):
        for way in (0, 1):
            by_copy(a, step, way, True).wait_recv()
            if step < 4:
                by_copy(a, step + 1, way, False).start()
        bx_start(a, *((-step, step) if step < 4 else (4,)))

    def start_rings(a):
        for r in (2, 3):
            z_arrival(a, r).wait_recv()
        for way in (0, 1):
            by_copy(a, 1, way, False).start()
        bx_start(a, 0)
        for r in (1, 0):
            def act(r=r):
                z_arrival(a, r).wait_recv()
                for way in (0, 1):
                    a_copy(a, r, 1, way, False).start()
            when_active(r, act)

    def round_of(a, number):
        if number == 0:
            start_rings(a)
        elif number == 1:
            by_move(a, 1)
        elif number == 2:
            by_move(a, 2)
            bx_move(a, 1, 0)
            a_move(a, 1)
        elif number == 3:
            by_move(a, 3)
            bx_move(a, 1, -1, 1)
        elif number == 4:
            by_move(a, 4)
            a_move(a, 2)
            bx_move(a, 1, -2, 2)
        elif number == 5:
            bx_move(a, 1, -3, 3)
            a_move(a, 3)
            bx_move(a, 1, 4)
        else:
            bx_move(a, 2, 0, -1, 1, -2, 2, -3, 3, 4)
            a_move(a, 4)

    def pass_heads(a, distances):
        for s in distances:
            head_copy(a, s, True).wait_recv()
            share_copy(a, s, False).start()

    def finish_tokens(a):
        for s in range(NZ):
            share_copy(a, s, True).wait_recv()

        @pl.when(is_source)
        def _():
            own_tokens(a).wait()

    def drain_transfers(a):
        @pl.when(is_source)
        def _():
            for s in range(1, NZ):
                z_copy(a, s).wait_send()
        for s in range(1, NZ):
            head_copy(a, s, False).wait_send()
            if a == TRAIN:
                meta_copy(s, False).wait_send()
        for s in range(NZ):
            share_copy(a, s, False).wait_send()
        for way in (0, 1):
            for step in range(1, 5):
                by_copy(a, step, way, False).wait_send()
                a_copy(a, 1, step, way, False).wait_send()
            for far in range(NY):
                for step in (1, 2):
                    bx_copy(a, far, step, way, False).wait_send()

        @pl.when(jnp.logical_not(is_source))
        def _():
            for way in (0, 1):
                for step in range(1, 5):
                    a_copy(a, 0, step, way, False).wait_send()

    def drain_home():
        for q in range(NZ):
            home_copy(q, False).wait_send()

    for a in (TRAIN, REF):
        @pl.when(is_source)
        def _():
            for s in (5, 2, 6, 1, 3, 7, 4):
                z_copy(a, s).start()
            own_tokens(a).start()
        if a == TRAIN:
            own_meta.start()
            for s in range(1, NZ):
                meta_copy(s, False).start()
        own_rows(a).start()
        for s in FAR_FIRST:
            head_copy(a, s, False).start()
    for q in range(NZ):
        home_local(q).start()
        home_copy(q, False).start()
    zero_stats = jnp.zeros((16, LANES), f32)
    for a in (REF, TRAIN):
        stats[a, 0] = zero_stats

    for number in range(4):
        round_of(TRAIN, number)
    own_rows(TRAIN).wait()
    share_copy(TRAIN, 0, False).start()
    round_of(TRAIN, 4)
    round_of(REF, 0)
    pass_heads(TRAIN, (1, 7, 2, 6))
    round_of(TRAIN, 5)
    round_of(REF, 1)
    pass_heads(TRAIN, (3, 5, 4))
    round_of(TRAIN, 6)
    own_meta.wait()
    for s in range(1, NZ):
        meta_copy(s, True).wait_recv()
    finish_tokens(TRAIN)

    row = lax.broadcasted_iota(jnp.int32, (BOTH, TOK), 0)
    within = row % ROWS
    chip = v // 2
    row_id = (2 * chip + row // ROWS) * 1008 + z * ROWS - 16 * (z // 7) + within
    valid = jnp.logical_or(within >= 16, z < 7)

    def hits(slot):
        target = lax.shift_right_logical(meta_all[4 * c + slot], 1)
        return jnp.logical_and(row_id == target, valid)

    def local_stats(a, slots):
        for r in slots:
            slot = (z + r) % 4
            table = lax.dot_general(
                gbuf[a], xbuf[a, TOK * r:TOK * (r + 1), :], LAST, preferred_element_type=f32
            )
            if a == TRAIN:
                logits[r] = table
            top = jnp.max(jnp.where(valid, table, -jnp.inf), axis=0, keepdims=True)
            parts = jnp.where(valid, jnp.exp(table - top), 0.0)
            picked = jnp.where(hits(slot), table, 0.0)
            stats[a, 0, pl.ds(slot, 1), :TOK] = top
            stats[a, 0, pl.ds(4 + slot, 1), :TOK] = jnp.sum(parts, axis=0, keepdims=True)
            stats[a, 0, pl.ds(8 + slot, 1), :TOK] = jnp.sum(picked, axis=0, keepdims=True)

    levels = (
        (z_peers, zstat, tz_send, tz_recv),
        (x_peers, xstat, tx_send, tx_recv),
        (y_peers, ystat, ty_send, ty_recv),
    )

    def stat_copies(a, level):
        peers, buf, send, recv = levels[level]
        return [
            remote(stats.at[a, level], buf.at[a, s], send.at[a, s], recv.at[a, s], peers[s + 1])
            for s in range(len(peers) - 1)
        ]

    def stat_send(a, level):
        for copy in stat_copies(a, level):
            copy.start()

    def stat_merge(a, level):
        copies = stat_copies(a, level)
        for copy in copies:
            copy.wait_recv()
        blocks = [stats[a, level]] + [levels[level][1][a, s] for s in range(len(copies))]
        top = functools.reduce(jnp.maximum, [b[0:4] for b in blocks])
        total = sum(b[4:8] * jnp.exp(b[0:4] - top) for b in blocks)
        picked = sum(b[8:12] for b in blocks)
        merged = jnp.concatenate([top, total, picked, jnp.zeros_like(top)], axis=0)
        if level < 2:
            stats[a, level + 1] = merged
        else:
            both[a, c] = merged

    def stat_share(a, arriving):
        part = both.at[a, 1 - c if arriving else c]
        return remote(part, part, tc_send.at[a], tc_recv.at[a], sibling)

    def drain_stats(a):
        for level in range(3):
            for copy in stat_copies(a, level):
                copy.wait_send()
        stat_share(a, False).wait_send()

    local_stats(TRAIN, range(4))
    stat_send(TRAIN, 0)
    round_of(REF, 2)
    stat_merge(TRAIN, 0)
    stat_send(TRAIN, 1)
    round_of(REF, 3)
    stat_merge(TRAIN, 1)
    stat_send(TRAIN, 2)
    own_rows(REF).wait()
    share_copy(REF, 0, False).start()
    stat_merge(TRAIN, 2)
    stat_share(TRAIN, False).start()

    upper = (
        lax.broadcasted_iota(jnp.int32, (TOK, TOK), 0)
        <= lax.broadcasted_iota(jnp.int32, (TOK, TOK), 1)
    ).astype(jnp.bfloat16)
    place = lax.broadcasted_iota(jnp.int32, (SLOT, TOK), 0)

    def choose(weight, place):
        count = jnp.dot(
            jnp.broadcast_to(weight, (8, TOK)).astype(jnp.bfloat16), upper,
            preferred_element_type=f32,
        )[0:1].astype(jnp.int32)
        return jnp.logical_and(place == count - 1, weight != 0)

    def slopes(b):
        for slot in (2 * b, 2 * b + 1):
            pick = choose(meta_all[4 * c + slot] & 1, place).astype(jnp.bfloat16)
            top = both[TRAIN, c, slot:slot + 1, :TOK]
            total = both[TRAIN, c, 4 + slot:5 + slot, :TOK]
            share = jnp.exp(logits[(slot + 4 - z % 4) % 4] - top) / total
            slope = jnp.where(valid, loss_scale * (share - hits(slot).astype(f32)), 0.0)
            rows = lax.dot_general(
                pick, slope.astype(jnp.bfloat16), LAST, preferred_element_type=f32
            )
            start = SLOT * (slot - 2 * b)
            gathered[z, b, start:start + SLOT, :] = rows.astype(jnp.bfloat16)

    def e_copy(b, step, way, arriving):
        rows = pl.ds(0, PAIR) if step < 4 else pl.ds(SLOT * way, SLOT)
        part = gathered.at[(z + back_of(step, way, arriving) + NZ) % NZ, b, rows, :]
        index = (b, step - 1, way)
        return remote(part, part, ez_send.at[index], ez_recv.at[index], around(z_peers, way))

    def e_move(b, step):
        for way in (0, 1):
            if step:
                e_copy(b, step, way, True).wait_recv()
            if step < 4:
                e_copy(b, step + 1, way, False).start()

    def x_copy(b, s):
        return remote(
            grad.at[b, (x + s) % NX], xgrad.at[b, s - 1], gx_send.at[b, s - 1],
            gx_recv.at[b, s - 1], x_peers[s],
        )

    def turned_part(b, q):
        return turned.at[b, q // 4, aligned((q % 4) * 32, 32, 32), :]

    def y_copy(b, s):
        return remote(
            turned_part(b, (y + s) % NY), ygrad.at[b, s - 1], gy_send.at[b, s - 1],
            gy_recv.at[b, s - 1], y_peers[s],
        )

    def final_copy(b):
        return remote(
            summed.at[b], piece.at[aligned((y % 2) * 32, 32, 32), :], f_send.at[b],
            f_recv.at[y % 2], dests[b],
        )

    def final_stay(b):
        return pltpu.make_async_copy(
            summed.at[b], piece.at[aligned((y % 2) * 32, 32, 32), :], local_sem.at[5 + b]
        )

    def multiply(b):
        columns = jnp.concatenate([gathered[q, b] for q in range(NZ)], axis=1)
        for q in range(NX):
            grad[b, q] = jnp.dot(
                columns, home[:, 128 * q:128 * (q + 1)], preferred_element_type=f32
            )
        for s in (2, 1, 3):
            x_copy(b, s).start()

    def turn(b):
        for s in range(1, NX):
            x_copy(b, s).wait_recv()
        total = grad[b, x] + xgrad[b, 0] + xgrad[b, 1] + xgrad[b, 2]
        for i in (0, 1):
            block = jnp.concatenate(
                [total[SLOT * i:SLOT * (i + 1)], jnp.zeros((128 - SLOT, 128), f32)], axis=0
            )
            turned[b, i] = block.T
        for s in FAR_FIRST:
            y_copy(b, s).start()

    def hand_over(b):
        for s in range(1, NY):
            y_copy(b, s).wait_recv()
        summed[b] = turned_part(b, y)[...] + sum(ygrad[b, s] for s in range(NY - 1))

        @pl.when(jnp.logical_not(is_here(dests[b])))
        def _():
            final_copy(b).start()

        @pl.when(is_here(dests[b]))
        def _():
            final_stay(b).start()
            final_stay(b).wait()

    def drain_grads():
        for b in (0, 1):
            for way in (0, 1):
                for step in range(1, 5):
                    e_copy(b, step, way, False).wait_send()
            for s in range(1, NX):
                x_copy(b, s).wait_send()
            for s in range(1, NY):
                y_copy(b, s).wait_send()

            @pl.when(jnp.logical_not(is_here(dests[b])))
            def _():
                final_copy(b).wait_send()

    slopes(0)
    e_move(0, 0)
    slopes(1)
    e_move(1, 0)
    round_of(REF, 4)
    e_move(0, 1)
    pass_heads(REF, (1, 7, 2))
    e_move(1, 1)
    e_move(0, 2)
    round_of(REF, 5)
    pass_heads(REF, (6, 3))
    e_move(1, 2)
    e_move(0, 3)
    pass_heads(REF, (5, 4))
    e_move(1, 3)
    for q in range(NZ):
        home_local(q).wait()
        home_copy(q, True).wait_recv()
    e_move(0, 4)
    multiply(0)
    round_of(REF, 6)
    finish_tokens(REF)
    local_stats(REF, (0, 1))
    e_move(1, 4)
    multiply(1)
    local_stats(REF, (2, 3))
    stat_send(REF, 0)
    turn(0)
    turn(1)
    stat_merge(REF, 0)
    stat_send(REF, 1)
    hand_over(0)
    hand_over(1)
    stat_merge(REF, 1)
    stat_send(REF, 2)
    for h in (0, 1):
        @pl.when(jnp.logical_not(is_here(origins[h])))
        def _():
            part = piece.at[pl.ds(32 * h, 32), :]
            remote(part, part, f_send.at[0], f_recv.at[h], sibling).wait_recv()
    own_place = choose(
        meta_all[z] & 1, lax.broadcasted_iota(jnp.int32, (128, TOK), 0)
    ).astype(f32)
    grad_out[...] = jnp.dot(
        piece[...], own_place, precision=lax.Precision.HIGHEST, preferred_element_type=f32
    )
    stat_merge(REF, 2)
    stat_share(REF, False).start()
    for a in (TRAIN, REF):
        stat_share(a, True).wait_recv()

    def cross(block, first, count):
        top = block[pl.ds(first, count), :TOK]
        total = block[pl.ds(4 + first, count), :TOK]
        return jnp.log(total) + top - block[pl.ds(8 + first, count), :TOK]

    excess_out[...] = cross(both.at[TRAIN, z // 4], z % 4, 1) - cross(
        both.at[REF, z // 4], z % 4, 1
    )
    loss = jnp.zeros((1, 1), f32)
    for h in (0, 1):
        weight = jnp.concatenate([meta_all[4 * h + i] & 1 for i in range(4)], axis=0)
        loss = loss + jnp.sum(
            weight.astype(f32) * cross(both.at[TRAIN, h], 0, 4), axis=(0, 1), keepdims=True
        )
    loss_out[...] = jnp.broadcast_to(loss / (NZ * SEL), loss_out.shape)

    for a in (REF, TRAIN):
        drain_transfers(a)
        drain_stats(a)
    drain_home()
    drain_grads()


def fused(hidden_ref, hidden_train, head_ref, head_train, meta):
    anywhere = pl.BlockSpec(memory_space=pl.ANY)
    vmem = pl.BlockSpec(memory_space=pltpu.VMEM)
    dma = pltpu.SemaphoreType.DMA
    sds = jax.ShapeDtypeStruct
    f32, bf16 = jnp.float32, jnp.bfloat16
    buf = pltpu.VMEM
    pairs = [
        (2, NZ - 1), (2, 4), (NZ - 1,), (NZ - 1,), (2, NZ - 1), (2, NZ - 1), (2, NZ), (2, NZ),
        (NZ,), (NZ,), (NZ,), (2, 2, 4, 2), (2, 2, 4, 2), (2, 4, 2), (2, 4, 2),
        (2, NY, 2, 2), (2, NY, 2, 2),
        (2, NZ - 1), (2, NZ - 1), (2, NX - 1), (2, NX - 1), (2, NY - 1), (2, NY - 1), (2,), (2,),
        (2, 4, 2), (2, 4, 2), (2, NX - 1), (2, NX - 1), (2, NY - 1), (2, NY - 1), (2,), (2,),
    ]
    return pl.pallas_call(
        kernel,
        out_shape=[sds((64, TOK), f32), sds((1, TOK), f32), sds((1, 128), f32)],
        in_specs=[anywhere] * 5,
        out_specs=[vmem] * 3,
        scratch_shapes=[
            buf((NZ, 1, TOK), jnp.int32), buf((2, 2, 16, LANES), f32),
            buf((2, 4 * TOK, WIDTH), bf16), buf((2, BOTH, WIDTH), bf16),
            buf((NZ * BOTH, FEAT), bf16), buf((4, BOTH, TOK), f32),
            buf((2, 3, 16, LANES), f32), buf((2, NZ - 1, 16, LANES), f32),
            buf((2, NX - 1, 16, LANES), f32), buf((2, NY - 1, 16, LANES), f32),
            buf((NZ, 2, PAIR, BOTH), bf16), buf((2, NX, PAIR, 128), f32),
            buf((2, NX - 1, PAIR, 128), f32), buf((2, 2, 128, 128), f32),
            buf((2, NY - 1, 32, 128), f32), buf((2, 32, 128), f32), buf((64, 128), f32),
            dma((7,)), *[dma(shape) for shape in pairs],
        ],
        compiler_params=pltpu.CompilerParams(
            collective_id=0, has_side_effects=True, vmem_limit_bytes=60 * 1024 * 1024
        ),
        name="fused",
    )(hidden_ref, hidden_train, head_ref, head_train, meta)


def body(hidden_ref, hidden_train, head_ref, head_train, targets, mask):
    meta = (2 * targets + mask).reshape(1, TOK)
    hidden_grad, excess, loss = fused(hidden_ref, hidden_train, head_ref, head_train, meta)
    return (excess.reshape(TOK), loss[0, 0], hidden_grad)


def solution(mesh):
    in_specs = (P("dp", None), P("dp", None), P("vocab", "dp"), P("vocab", "dp"), P("dp"), P("dp"))
    out_specs = (P("dp"), P(), P("vocab", "dp"))
    return jax.shard_map(body, mesh=mesh, in_specs=in_specs, out_specs=out_specs, check_vma=False)
```

```python
import functools

import jax
import jax.numpy as jnp
from jax import lax
from jax.experimental import pallas as pl
from jax.experimental.pallas import tpu as pltpu
from jax.sharding import PartitionSpec as P

MESH = pl.DeviceIdType.MESH
NX, NY, NZ = 4, 8, 8
loss_scale = 64.0
TOK = 160
SEL = 100
SLOT = 112
ROWS = 128
PIECE = 128
FEAT = 512
WIDTH = 4096
PAIR = 2 * SLOT
LANES = 256
BOTH = 2 * ROWS
FAR_FIRST = (4, 3, 5, 2, 6, 1, 7)
NEAR_FIRST = (1, 7, 2, 6, 3, 5, 4)
REF_FIRST = (2, 6, 1, 7)
REF_LATER = (3, 5, 4)
LAST = (((1,), (1,)), ((), ()))
REF, TRAIN = 0, 1


def coords():
    z = lax.axis_index("dp")
    v = lax.axis_index("vocab")
    return v // 16, (v // 2) % NY, z, v % 2


def vocab_index(x, y, c):
    return (x * NY + y) * 2 + c


def remote(src, dst, send_sem, recv_sem, device):
    return pltpu.make_async_remote_copy(
        src_ref=src, dst_ref=dst, send_sem=send_sem, recv_sem=recv_sem,
        device_id=device, device_id_type=MESH,
    )


def aligned(start, size, step):
    return pl.ds(pl.multiple_of(start, step), size)


def kernel(
    hid_ref, hid_train, head_ref, head_train, targets, mask,
    grad_out, excess_out, loss_out,
    meta, meta_all, stats_t, zstat_t, xstat_t, ystat_t, both_t,
    stats_r, zstat_r, xstat_r, ystat_r, both_r, xbuf, gbuf, home, logits, gathered, grad, xgrad, turned, ygrad, summed, piece,
    local_sem, z_send, z_recv, m_send, m_recv, w_send, w_recv, s_send, s_recv,
    h_local, h_send, h_recv, ax_send, ax_recv, ay_send, ay_recv, by_send, by_recv, bx_send, bx_recv,
    tz_send, tz_recv, tx_send, tx_recv, ty_send, ty_recv, tc_send, tc_recv,
    ez_send, ez_recv, gx_send, gx_recv, gy_send, gy_recv, f_send, f_recv,
):
    f32 = jnp.float32
    x, y, z, c = coords()
    v = vocab_index(x, y, c)
    sibling = (z, vocab_index(x, y, 1 - c))
    z_peers = [None] + [((z + s) % NZ, v) for s in range(1, NZ)]
    x_peers = [None] + [(z, vocab_index((x + s) % NX, y, c)) for s in range(1, NX)]
    y_peers = [None] + [(z, vocab_index(x, (y + s) % NY, c)) for s in range(1, NY)]
    dests = [(4 * c + 2 * b + y // 4, 8 * z + 2 * x + (y % 4) // 2) for b in (0, 1)]
    origins = [
        (v // 8, vocab_index((v % 8) // 2, 4 * (z % 2) + 2 * (v % 2) + h, z // 4)) for h in (0, 1)
    ]

    def is_here(device):
        return jnp.logical_and(device[0] == z, device[1] == v)

    barrier = pltpu.get_barrier_semaphore()
    friends = z_peers[1:] + x_peers[1:] + y_peers[1:] + [sibling]
    for device in friends:
        pl.semaphore_signal(barrier, inc=1, device_id=device, device_id_type=MESH)
    expected = len(friends) + 4
    for device in dests + origins:
        expected = expected - is_here(device).astype(jnp.int32)

        @pl.when(jnp.logical_not(is_here(device)))
        def _():
            pl.semaphore_signal(barrier, inc=1, device_id=device, device_id_type=MESH)

    pl.semaphore_wait(barrier, expected)

    meta[...] = 2 * targets[...] + mask[...]

    is_source = z // 4 == c
    hid = (hid_ref, hid_train)
    heads = (head_ref, head_train)

    def when_active(r, act):
        if r:
            act()
        else:
            pl.when(jnp.logical_not(is_source))(act)

    def z_columns(r):
        if r < 2:
            return aligned((y * NX + x) * PIECE, PIECE, PIECE)
        return aligned((x * NY + y) * PIECE, PIECE, PIECE)

    def z_copy(a, s):
        r = -s % 4
        columns = z_columns(r)
        return remote(
            hid[a].at[:, columns], xbuf.at[a, pl.ds(TOK * r, TOK), columns],
            z_send.at[a, s - 1], z_recv.at[a, r], z_peers[s],
        )

    def z_arrival(a, r):
        part = xbuf.at[a, pl.ds(TOK * r, TOK), z_columns(r)]
        return remote(part, part, z_send.at[a, 0], z_recv.at[a, r], sibling)

    def own_tokens(a):
        return pltpu.make_async_copy(hid[a], xbuf.at[a, pl.ds(0, TOK), :], local_sem.at[a])

    def meta_copy(s, arriving):
        source = (z + NZ - s) % NZ if arriving else z
        return remote(meta, meta_all.at[source], m_send.at[s - 1], m_recv.at[s - 1], z_peers[s])

    def row_block(q):
        return aligned(q * ROWS - 16 * (q // 7), ROWS, 16)

    def head_part(a, core, source):
        return gbuf.at[a, aligned(ROWS * core, ROWS, ROWS), aligned(source * FEAT, FEAT, FEAT)]

    def head_copy(a, s, arriving):
        source = (z + NZ - s) % NZ if arriving else z
        return remote(
            heads[a].at[row_block((z + s) % NZ), :], head_part(a, c, source),
            w_send.at[a, s - 1], w_recv.at[a, s - 1], z_peers[s],
        )

    def own_rows(a):
        return pltpu.make_async_copy(
            heads[a].at[row_block(z), :], head_part(a, c, z), local_sem.at[2 + a]
        )

    def share_copy(a, s, arriving):
        part = head_part(a, 1 - c if arriving else c, (z + NZ - s) % NZ)
        return remote(part, part, s_send.at[a, s], s_recv.at[a, s], sibling)

    own_meta = pltpu.make_async_copy(meta, meta_all.at[z], local_sem.at[4])

    def home_local(q):
        return pltpu.make_async_copy(
            head_train.at[row_block(q), :], home.at[aligned(q * BOTH + c * ROWS, ROWS, ROWS), :],
            h_local.at[q],
        )

    def home_copy(q, arriving):
        core = 1 - c if arriving else c
        return remote(
            head_train.at[row_block(q), :], home.at[aligned(q * BOTH + core * ROWS, ROWS, ROWS), :],
            h_send.at[q], h_recv.at[q], sibling,
        )

    def around(peers, way):
        return peers[1 if way == 0 else len(peers) - 1]

    def back_of(step, way, arriving):
        back = step if arriving else step - 1
        return -back if way == 0 else back

    def ax_copy(a, r, step, way, arriving):
        block = y * NX + (x + back_of(step, way, arriving) + NX) % NX
        rows = pl.ds(TOK * r, TOK) if step < 2 else pl.ds(TOK * r + 80 * way, 80)
        part = xbuf.at[a, rows, aligned(block * PIECE, PIECE, PIECE)]
        index = (a, r, step - 1, way)
        return remote(part, part, ax_send.at[index], ax_recv.at[index], around(x_peers, way))

    def a_copy(a, r, step, way, arriving):
        block = (y + back_of(step, way, arriving) + NY) % NY
        rows = pl.ds(TOK * r, TOK) if step < 4 else pl.ds(TOK * r + 80 * way, 80)
        part = xbuf.at[a, rows, aligned(block * FEAT, FEAT, FEAT)]
        index = (a, r, step - 1, way)
        return remote(part, part, ay_send.at[index], ay_recv.at[index], around(y_peers, way))

    def b_rows(step, last, way):
        return pl.ds(2 * TOK, 2 * TOK) if step < last else pl.ds(2 * TOK + TOK * way, TOK)

    def by_copy(a, step, way, arriving):
        block = x * NY + (y + back_of(step, way, arriving) + NY) % NY
        part = xbuf.at[a, b_rows(step, 4, way), aligned(block * PIECE, PIECE, PIECE)]
        index = (a, step - 1, way)
        return remote(part, part, by_send.at[index], by_recv.at[index], around(y_peers, way))

    def bx_copy(a, far, step, way, arriving):
        block = ((x + back_of(step, way, arriving) + NX) % NX) * NY + (y + far) % NY
        part = xbuf.at[a, b_rows(step, 2, way), aligned(block * PIECE, PIECE, PIECE)]
        index = (a, far, step - 1, way)
        return remote(part, part, bx_send.at[index], bx_recv.at[index], around(x_peers, way))

    def ax_move(a, step):
        for r in (1, 0):
            def act(r=r):
                for way in (0, 1):
                    if step:
                        ax_copy(a, r, step, way, True).wait_recv()
                    if step < 2:
                        ax_copy(a, r, step + 1, way, False).start()
                if step == 2:
                    for way in (0, 1):
                        a_copy(a, r, 1, way, False).start()
            when_active(r, act)

    def a_move(a, step):
        for r in (1, 0):
            def act(r=r):
                for way in (0, 1):
                    a_copy(a, r, step, way, True).wait_recv()
                    if step < 4:
                        a_copy(a, r, step + 1, way, False).start()
            when_active(r, act)

    def bx_start(a, *fars):
        for far in fars:
            for way in (0, 1):
                bx_copy(a, far % NY, 1, way, False).start()

    def bx_move(a, step, *fars):
        for far in fars:
            for way in (0, 1):
                bx_copy(a, far % NY, step, way, True).wait_recv()
                if step == 1:
                    bx_copy(a, far % NY, 2, way, False).start()

    def by_move(a, step):
        for way in (0, 1):
            by_copy(a, step, way, True).wait_recv()
            if step < 4:
                by_copy(a, step + 1, way, False).start()
        bx_start(a, *((-step, step) if step < 4 else (4,)))

    def round_of(a, number):
        if number == 0:
            for r in (2, 3):
                z_arrival(a, r).wait_recv()
            for way in (0, 1):
                by_copy(a, 1, way, False).start()
            bx_start(a, 0)
            for r in (1, 0):
                when_active(r, lambda r=r: z_arrival(a, r).wait_recv())
            ax_move(a, 0)
        elif number == 1:
            by_move(a, 1)
            ax_move(a, 1)
        elif number == 2:
            by_move(a, 2)
            ax_move(a, 2)
            bx_move(a, 1, 0)
        elif number == 3:
            by_move(a, 3)
            bx_move(a, 1, -1, 1)
        elif number == 4:
            by_move(a, 4)
            a_move(a, 1)
            bx_move(a, 1, -2, 2)
        elif number == 5:
            a_move(a, 2)
            bx_move(a, 1, -3, 3, 4)
            a_move(a, 3)
        else:
            bx_move(a, 2, 0, -1, 1, -2, 2, -3, 3, 4)
            a_move(a, 4)

    def pass_heads(a, distances):
        for s in distances:
            head_copy(a, s, True).wait_recv()
            share_copy(a, s, False).start()

    def finish_tokens(a):
        for s in range(NZ):
            share_copy(a, s, True).wait_recv()

        @pl.when(is_source)
        def _():
            own_tokens(a).wait()

    def drain_transfers(a):
        @pl.when(is_source)
        def _():
            for s in range(1, NZ):
                z_copy(a, s).wait_send()
        for s in range(1, NZ):
            head_copy(a, s, False).wait_send()
            if a == TRAIN:
                meta_copy(s, False).wait_send()
        for s in range(NZ):
            share_copy(a, s, False).wait_send()
        for way in (0, 1):
            for step in range(1, 5):
                by_copy(a, step, way, False).wait_send()
            for far in range(NY):
                for step in (1, 2):
                    bx_copy(a, far, step, way, False).wait_send()
        for r in (0, 1):
            def act(r=r):
                for way in (0, 1):
                    for step in (1, 2):
                        ax_copy(a, r, step, way, False).wait_send()
                    for step in range(1, 5):
                        a_copy(a, r, step, way, False).wait_send()
            when_active(r, act)

    def drain_home():
        for q in range(NZ):
            home_copy(q, False).wait_send()

    def send_tokens(a):
        @pl.when(is_source)
        def _():
            for s in (5, 2, 6, 1, 3, 7, 4):
                z_copy(a, s).start()
            own_tokens(a).start()

    def send_heads(a, distances):
        for s in distances:
            head_copy(a, s, False).start()

    send_tokens(TRAIN)
    own_meta.start()
    for s in range(1, NZ):
        meta_copy(s, False).start()
    own_rows(TRAIN).start()
    own_rows(REF).start()
    stats_t[0] = jnp.zeros((8, LANES), f32)
    stats_r[0] = jnp.zeros((16, LANES), f32)
    round_of(TRAIN, 0)
    send_heads(TRAIN, FAR_FIRST)
    round_of(TRAIN, 1)
    own_rows(TRAIN).wait()
    share_copy(TRAIN, 0, False).start()
    own_rows(REF).wait()
    share_copy(REF, 0, False).start()
    round_of(TRAIN, 2)
    for q in range(NZ):
        home_local(q).start()
        home_copy(q, False).start()
    for number in (3, 4, 5):
        round_of(TRAIN, number)
    pass_heads(TRAIN, NEAR_FIRST)
    send_tokens(REF)
    send_heads(REF, FAR_FIRST)
    round_of(REF, 0)
    round_of(TRAIN, 6)
    own_meta.wait()
    for s in range(1, NZ):
        meta_copy(s, True).wait_recv()
    finish_tokens(TRAIN)
    round_of(REF, 1)

    row = lax.broadcasted_iota(jnp.int32, (BOTH, TOK), 0)
    within = row % ROWS
    chip = v // 2
    row_id = (2 * chip + row // ROWS) * 1008 + z * ROWS - 16 * (z // 7) + within
    valid = jnp.logical_or(within >= 16, z < 7)

    def hits(slot):
        target = lax.shift_right_logical(meta_all[4 * c + slot], 1)
        return jnp.logical_and(row_id == target, valid)

    def local_stats(a, slots):
        for r in slots:
            slot = (z + r) % 4
            table = lax.dot_general(
                gbuf[a], xbuf[a, TOK * r:TOK * (r + 1), :], LAST, preferred_element_type=f32
            )
            if a == TRAIN:
                logits[r] = table
            top = jnp.max(jnp.where(valid, table, -jnp.inf), axis=0, keepdims=True)
            parts = jnp.where(valid, jnp.exp(table - top), 0.0)
            picked = jnp.where(hits(slot), table, 0.0)
            mine = (stats_r, stats_t)[a]
            mine[0, pl.ds(slot, 1), :TOK] = top
            mine[0, pl.ds(4 + slot, 1), :TOK] = jnp.sum(parts, axis=0, keepdims=True)
            stats_r[0, pl.ds(8 + 4 * a + slot, 1), :TOK] = jnp.sum(picked, axis=0, keepdims=True)

    sums = (
        ((stats_r, zstat_r, xstat_r, ystat_r), both_r), ((stats_t, zstat_t, xstat_t, ystat_t), both_t)
    )
    hops = ((z_peers, tz_send, tz_recv), (x_peers, tx_send, tx_recv), (y_peers, ty_send, ty_recv))

    def stat_copies(a, level):
        peers, send, recv = hops[level]
        bufs = sums[a][0]
        return [
            remote(
                bufs[0].at[level], bufs[level + 1].at[s], send.at[a, s], recv.at[a, s], peers[s + 1]
            )
            for s in range(len(peers) - 1)
        ]

    def stat_send(a, level):
        for copy in stat_copies(a, level):
            copy.start()

    def stat_merge(a, level):
        bufs, result = sums[a]
        copies = stat_copies(a, level)
        for copy in copies:
            copy.wait_recv()
        blocks = [bufs[0][level]] + [bufs[level + 1][s] for s in range(len(copies))]
        top = functools.reduce(jnp.maximum, [b[0:4] for b in blocks])
        total = sum(b[4:8] * jnp.exp(b[0:4] - top) for b in blocks)
        merged = jnp.concatenate([top, total] + [sum(b[8:] for b in blocks)] * (1 - a), axis=0)
        if level < 2:
            bufs[0][level + 1] = merged
        else:
            result[c] = merged

    def stat_share(a, arriving):
        part = sums[a][1].at[1 - c if arriving else c]
        return remote(part, part, tc_send.at[a], tc_recv.at[a], sibling)

    def drain_stats(a):
        for level in range(3):
            for copy in stat_copies(a, level):
                copy.wait_send()
        stat_share(a, False).wait_send()

    local_stats(TRAIN, range(4))
    stat_send(TRAIN, 0)
    round_of(REF, 2)
    stat_merge(TRAIN, 0)
    stat_send(TRAIN, 1)
    round_of(REF, 3)
    stat_merge(TRAIN, 1)
    stat_send(TRAIN, 2)
    round_of(REF, 4)
    pass_heads(REF, REF_FIRST)
    stat_merge(TRAIN, 2)
    stat_share(TRAIN, False).start()

    upper = (
        lax.broadcasted_iota(jnp.int32, (TOK, TOK), 0)
        <= lax.broadcasted_iota(jnp.int32, (TOK, TOK), 1)
    ).astype(jnp.bfloat16)
    place = lax.broadcasted_iota(jnp.int32, (SLOT, TOK), 0)

    def choose(weight, place):
        count = jnp.dot(
            jnp.broadcast_to(weight, (8, TOK)).astype(jnp.bfloat16), upper,
            preferred_element_type=f32,
        )[0:1].astype(jnp.int32)
        return jnp.logical_and(place == count - 1, weight != 0)

    def slopes(b):
        for slot in (2 * b, 2 * b + 1):
            pick = choose(meta_all[4 * c + slot] & 1, place).astype(jnp.bfloat16)
            top = both_t[c, slot:slot + 1, :TOK]
            total = both_t[c, 4 + slot:5 + slot, :TOK]
            share = jnp.exp(logits[(slot + 4 - z % 4) % 4] - top) / total
            slope = jnp.where(valid, loss_scale * (share - hits(slot).astype(f32)), 0.0)
            rows = lax.dot_general(
                pick, slope.astype(jnp.bfloat16), LAST, preferred_element_type=f32
            )
            start = SLOT * (slot - 2 * b)
            gathered[z, b, start:start + SLOT, :] = rows.astype(jnp.bfloat16)

    def e_copy(b, step, way, arriving):
        rows = pl.ds(0, PAIR) if step < 4 else pl.ds(SLOT * way, SLOT)
        part = gathered.at[(z + back_of(step, way, arriving) + NZ) % NZ, b, rows, :]
        index = (b, step - 1, way)
        return remote(part, part, ez_send.at[index], ez_recv.at[index], around(z_peers, way))

    def e_move(b, step):
        for way in (0, 1):
            if step:
                e_copy(b, step, way, True).wait_recv()
            if step < 4:
                e_copy(b, step + 1, way, False).start()

    def x_copy(b, s):
        return remote(
            grad.at[b, (x + s) % NX], xgrad.at[b, s - 1], gx_send.at[b, s - 1],
            gx_recv.at[b, s - 1], x_peers[s],
        )

    def turned_part(b, q):
        return turned.at[b, q // 4, aligned((q % 4) * 32, 32, 32), :]

    def y_copy(b, s):
        return remote(
            turned_part(b, (y + s) % NY), ygrad.at[b, s - 1], gy_send.at[b, s - 1],
            gy_recv.at[b, s - 1], y_peers[s],
        )

    def final_copy(b):
        return remote(
            summed.at[b], piece.at[aligned((y % 2) * 32, 32, 32), :], f_send.at[b],
            f_recv.at[y % 2], dests[b],
        )

    def final_stay(b):
        return pltpu.make_async_copy(
            summed.at[b], piece.at[aligned((y % 2) * 32, 32, 32), :], local_sem.at[5 + b]
        )

    def multiply(b):
        columns = jnp.concatenate([gathered[q, b] for q in range(NZ)], axis=1)
        for q in range(NX):
            grad[b, q] = jnp.dot(
                columns, home[:, 128 * q:128 * (q + 1)], preferred_element_type=f32
            )
        for s in (2, 1, 3):
            x_copy(b, s).start()

    def turn(b):
        for s in range(1, NX):
            x_copy(b, s).wait_recv()
        total = grad[b, x] + xgrad[b, 0] + xgrad[b, 1] + xgrad[b, 2]
        for i in (0, 1):
            block = jnp.concatenate(
                [total[SLOT * i:SLOT * (i + 1)], jnp.zeros((128 - SLOT, 128), f32)], axis=0
            )
            turned[b, i] = block.T
        for s in FAR_FIRST:
            y_copy(b, s).start()

    def hand_over(b):
        for s in range(1, NY):
            y_copy(b, s).wait_recv()
        summed[b] = turned_part(b, y)[...] + sum(ygrad[b, s] for s in range(NY - 1))

        @pl.when(jnp.logical_not(is_here(dests[b])))
        def _():
            final_copy(b).start()

        @pl.when(is_here(dests[b]))
        def _():
            final_stay(b).start()
            final_stay(b).wait()

    def drain_grads():
        for b in (0, 1):
            for way in (0, 1):
                for step in range(1, 5):
                    e_copy(b, step, way, False).wait_send()
            for s in range(1, NX):
                x_copy(b, s).wait_send()
            for s in range(1, NY):
                y_copy(b, s).wait_send()

            @pl.when(jnp.logical_not(is_here(dests[b])))
            def _():
                final_copy(b).wait_send()

    slopes(0)
    e_move(0, 0)
    slopes(1)
    e_move(1, 0)
    e_move(0, 1)
    e_move(1, 1)
    round_of(REF, 5)
    e_move(0, 2)
    e_move(1, 2)
    pass_heads(REF, REF_LATER)
    e_move(0, 3)
    e_move(1, 3)
    for q in range(NZ):
        home_local(q).wait()
        home_copy(q, True).wait_recv()
    e_move(0, 4)
    multiply(0)
    e_move(1, 4)
    multiply(1)
    round_of(REF, 6)
    finish_tokens(REF)
    local_stats(REF, range(4))
    stat_send(REF, 0)
    turn(0)
    turn(1)
    stat_merge(REF, 0)
    stat_send(REF, 1)
    hand_over(0)
    hand_over(1)
    stat_merge(REF, 1)
    stat_send(REF, 2)
    for h in (0, 1):
        @pl.when(jnp.logical_not(is_here(origins[h])))
        def _():
            part = piece.at[pl.ds(32 * h, 32), :]
            remote(part, part, f_send.at[0], f_recv.at[h], sibling).wait_recv()
    own_place = choose(
        meta_all[z] & 1, lax.broadcasted_iota(jnp.int32, (128, TOK), 0)
    ).astype(f32)
    grad_out[...] = jnp.dot(
        piece[...], own_place, precision=lax.Precision.HIGHEST, preferred_element_type=f32
    )
    stat_merge(REF, 2)
    stat_share(REF, False).start()
    for a in (TRAIN, REF):
        stat_share(a, True).wait_recv()

    def cross(a, h, first, count):
        block = sums[a][1].at[h]
        top = block[pl.ds(first, count), :TOK]
        total = block[pl.ds(4 + first, count), :TOK]
        return jnp.log(total) + top - both_r[h, pl.ds(8 + 4 * a + first, count), :TOK]

    excess_out[...] = cross(TRAIN, z // 4, z % 4, 1) - cross(REF, z // 4, z % 4, 1)
    loss = jnp.zeros((1, 1), f32)
    for h in (0, 1):
        weight = jnp.concatenate([meta_all[4 * h + i] & 1 for i in range(4)], axis=0)
        loss = loss + jnp.sum(
            weight.astype(f32) * cross(TRAIN, h, 0, 4), axis=(0, 1), keepdims=True
        )
    loss_out[...] = jnp.broadcast_to(loss / (NZ * SEL), loss_out.shape)

    for a in (REF, TRAIN):
        drain_transfers(a)
        drain_stats(a)
    drain_home()
    drain_grads()


def fused(hidden_ref, hidden_train, head_ref, head_train, targets, mask):
    anywhere = pl.BlockSpec(memory_space=pl.ANY)
    vmem = pl.BlockSpec(memory_space=pltpu.VMEM)
    dma = pltpu.SemaphoreType.DMA
    sds = jax.ShapeDtypeStruct
    f32, bf16 = jnp.float32, jnp.bfloat16
    buf = pltpu.VMEM
    pairs = [
        (2, NZ - 1), (2, 4), (NZ - 1,), (NZ - 1,), (2, NZ - 1), (2, NZ - 1), (2, NZ), (2, NZ),
        (NZ,), (NZ,), (NZ,), (2, 2, 2, 2), (2, 2, 2, 2), (2, 2, 4, 2), (2, 2, 4, 2), (2, 4, 2), (2, 4, 2),
        (2, NY, 2, 2), (2, NY, 2, 2),
        (2, NZ - 1), (2, NZ - 1), (2, NX - 1), (2, NX - 1), (2, NY - 1), (2, NY - 1), (2,), (2,),
        (2, 4, 2), (2, 4, 2), (2, NX - 1), (2, NX - 1), (2, NY - 1), (2, NY - 1), (2,), (2,),
    ]
    return pl.pallas_call(
        kernel,
        out_shape=[sds((64, TOK), f32), sds((1, TOK), f32), sds((1, 128), f32)],
        in_specs=[anywhere] * 4 + [vmem] * 2,
        out_specs=[vmem] * 3,
        scratch_shapes=[
            buf((1, TOK), jnp.int32), buf((NZ, 1, TOK), jnp.int32),
            *[
                buf((count, rows, LANES), f32)
                for rows in (8, 16) for count in (3, NZ - 1, NX - 1, NY - 1, 2)
            ],
            buf((2, 4 * TOK, WIDTH), bf16), buf((2, BOTH, WIDTH), bf16),
            buf((NZ * BOTH, FEAT), bf16), buf((4, BOTH, TOK), f32),
            buf((NZ, 2, PAIR, BOTH), bf16), buf((2, NX, PAIR, 128), f32),
            buf((2, NX - 1, PAIR, 128), f32), buf((2, 2, 128, 128), f32),
            buf((2, NY - 1, 32, 128), f32), buf((2, 32, 128), f32), buf((64, 128), f32),
            dma((7,)), *[dma(shape) for shape in pairs],
        ],
        compiler_params=pltpu.CompilerParams(
            collective_id=0, has_side_effects=True, vmem_limit_bytes=60 * 1024 * 1024
        ),
        name="fused",
    )(hidden_ref, hidden_train, head_ref, head_train, targets, mask)


def body(hidden_ref, hidden_train, head_ref, head_train, targets, mask):
    hidden_grad, excess, loss = fused(
        hidden_ref, hidden_train, head_ref, head_train,
        targets.reshape(1, TOK), mask.reshape(1, TOK),
    )
    return (excess.reshape(TOK), loss[0, 0], hidden_grad)


def solution(mesh):
    in_specs = (P("dp", None), P("dp", None), P("vocab", "dp"), P("vocab", "dp"), P("dp"), P("dp"))
    out_specs = (P("dp"), P(), P("vocab", "dp"))
    return jax.shard_map(body, mesh=mesh, in_specs=in_specs, out_specs=out_specs, check_vma=False)
```

```python
import functools

import jax
import jax.numpy as jnp
from jax import lax
from jax.experimental import pallas as pl
from jax.experimental.pallas import tpu as pltpu
from jax.sharding import PartitionSpec as P

MESH = pl.DeviceIdType.MESH
NX, NY, NZ = 4, 8, 8
loss_scale = 64.0
TOK = 160
SEL = 100
SLOT = 112
ROWS = 128
PIECE = 128
FEAT = 512
WIDTH = 4096
PAIR = 2 * SLOT
LANES = 256
BOTH = 2 * ROWS
FAR_FIRST = (4, 3, 5, 2, 6, 1, 7)
NEAR_FIRST = (1, 7, 2, 6, 3, 5, 4)
LAST = (((1,), (1,)), ((), ()))
REF, TRAIN = 0, 1


def coords():
    z = lax.axis_index("dp")
    v = lax.axis_index("vocab")
    return v // 16, (v // 2) % NY, z, v % 2


def vocab_index(x, y, c):
    return (x * NY + y) * 2 + c


def remote(src, dst, send_sem, recv_sem, device):
    return pltpu.make_async_remote_copy(
        src_ref=src, dst_ref=dst, send_sem=send_sem, recv_sem=recv_sem,
        device_id=device, device_id_type=MESH,
    )


def aligned(start, size, step):
    return pl.ds(pl.multiple_of(start, step), size)


def kernel(
    hid_ref, hid_train, head_ref, head_train, targets, mask,
    grad_out, excess_out, loss_out,
    meta, meta_all, stats_t, zstat_t, xstat_t, ystat_t, both_t,
    stats_r, zstat_r, xstat_r, ystat_r, both_r, xbuf, gbuf, home, logits, gathered, grad, xgrad, turned, ygrad, summed, piece,
    local_sem, z_send, z_recv, m_send, m_recv, w_send, w_recv, s_send, s_recv,
    h_local, h_send, h_recv, ax_send, ax_recv, ay_send, ay_recv, by_send, by_recv, bx_send, bx_recv,
    tz_send, tz_recv, tx_send, tx_recv, ty_send, ty_recv, tc_send, tc_recv,
    ez_send, ez_recv, gx_send, gx_recv, gy_send, gy_recv, f_send, f_recv,
):
    f32 = jnp.float32
    x, y, z, c = coords()
    v = vocab_index(x, y, c)
    sibling = (z, vocab_index(x, y, 1 - c))
    z_peers = [None] + [((z + s) % NZ, v) for s in range(1, NZ)]
    x_peers = [None] + [(z, vocab_index((x + s) % NX, y, c)) for s in range(1, NX)]
    y_peers = [None] + [(z, vocab_index(x, (y + s) % NY, c)) for s in range(1, NY)]
    dests = [(4 * c + 2 * b + y // 4, 8 * z + 2 * x + (y % 4) // 2) for b in (0, 1)]
    origins = [
        (v // 8, vocab_index((v % 8) // 2, 4 * (z % 2) + 2 * (v % 2) + h, z // 4)) for h in (0, 1)
    ]

    def is_here(device):
        return jnp.logical_and(device[0] == z, device[1] == v)

    barrier = pltpu.get_barrier_semaphore()
    friends = z_peers[1:] + x_peers[1:] + y_peers[1:] + [sibling]
    for device in friends:
        pl.semaphore_signal(barrier, inc=1, device_id=device, device_id_type=MESH)
    expected = len(friends) + 4
    for device in dests + origins:
        expected = expected - is_here(device).astype(jnp.int32)

        @pl.when(jnp.logical_not(is_here(device)))
        def _():
            pl.semaphore_signal(barrier, inc=1, device_id=device, device_id_type=MESH)

    pl.semaphore_wait(barrier, expected)

    meta[...] = 2 * targets[...] + mask[...]

    is_source = z // 4 == c
    hid = (hid_ref, hid_train)
    heads = (head_ref, head_train)

    def when_active(r, act):
        if r:
            act()
        else:
            pl.when(jnp.logical_not(is_source))(act)

    def z_columns(r):
        if r < 2:
            return aligned((y * NX + x) * PIECE, PIECE, PIECE)
        return aligned((x * NY + y) * PIECE, PIECE, PIECE)

    def z_copy(a, s):
        r = -s % 4
        columns = z_columns(r)
        return remote(
            hid[a].at[:, columns], xbuf.at[a, pl.ds(TOK * r, TOK), columns],
            z_send.at[a, s - 1], z_recv.at[a, r], z_peers[s],
        )

    def z_arrival(a, r):
        part = xbuf.at[a, pl.ds(TOK * r, TOK), z_columns(r)]
        return remote(part, part, z_send.at[a, 0], z_recv.at[a, r], sibling)

    def own_tokens(a):
        return pltpu.make_async_copy(hid[a], xbuf.at[a, pl.ds(0, TOK), :], local_sem.at[a])

    def meta_copy(s, arriving):
        source = (z + NZ - s) % NZ if arriving else z
        return remote(meta, meta_all.at[source], m_send.at[s - 1], m_recv.at[s - 1], z_peers[s])

    def row_block(q):
        return aligned(q * ROWS - 16 * (q // 7), ROWS, 16)

    def head_part(a, core, source):
        return gbuf.at[a, aligned(ROWS * core, ROWS, ROWS), aligned(source * FEAT, FEAT, FEAT)]

    def head_copy(a, s, arriving):
        source = (z + NZ - s) % NZ if arriving else z
        return remote(
            heads[a].at[row_block((z + s) % NZ), :], head_part(a, c, source),
            w_send.at[a, s - 1], w_recv.at[a, s - 1], z_peers[s],
        )

    def own_rows(a):
        return pltpu.make_async_copy(
            heads[a].at[row_block(z), :], head_part(a, c, z), local_sem.at[2 + a]
        )

    def share_copy(a, s, arriving):
        part = head_part(a, 1 - c if arriving else c, (z + NZ - s) % NZ)
        return remote(part, part, s_send.at[a, s], s_recv.at[a, s], sibling)

    own_meta = pltpu.make_async_copy(meta, meta_all.at[z], local_sem.at[4])

    def home_local(q):
        return pltpu.make_async_copy(
            head_train.at[row_block(q), :], home.at[aligned(q * BOTH + c * ROWS, ROWS, ROWS), :],
            h_local.at[q],
        )

    def home_copy(q, arriving):
        core = 1 - c if arriving else c
        return remote(
            head_train.at[row_block(q), :], home.at[aligned(q * BOTH + core * ROWS, ROWS, ROWS), :],
            h_send.at[q], h_recv.at[q], sibling,
        )

    def around(peers, way):
        return peers[1 if way == 0 else len(peers) - 1]

    def back_of(step, way, arriving):
        back = step if arriving else step - 1
        return -back if way == 0 else back

    def ax_copy(a, r, step, way, arriving):
        block = y * NX + (x + back_of(step, way, arriving) + NX) % NX
        rows = pl.ds(TOK * r, TOK) if step < 2 else pl.ds(TOK * r + 80 * way, 80)
        part = xbuf.at[a, rows, aligned(block * PIECE, PIECE, PIECE)]
        index = (a, r, step - 1, way)
        return remote(part, part, ax_send.at[index], ax_recv.at[index], around(x_peers, way))

    def a_copy(a, r, step, way, arriving):
        block = (y + back_of(step, way, arriving) + NY) % NY
        rows = pl.ds(TOK * r, TOK) if step < 4 else pl.ds(TOK * r + 80 * way, 80)
        part = xbuf.at[a, rows, aligned(block * FEAT, FEAT, FEAT)]
        index = (a, r, step - 1, way)
        return remote(part, part, ay_send.at[index], ay_recv.at[index], around(y_peers, way))

    def b_rows(step, last, way):
        return pl.ds(2 * TOK, 2 * TOK) if step < last else pl.ds(2 * TOK + TOK * way, TOK)

    def by_copy(a, step, way, arriving):
        block = x * NY + (y + back_of(step, way, arriving) + NY) % NY
        part = xbuf.at[a, b_rows(step, 4, way), aligned(block * PIECE, PIECE, PIECE)]
        index = (a, step - 1, way)
        return remote(part, part, by_send.at[index], by_recv.at[index], around(y_peers, way))

    def bx_copy(a, far, step, way, arriving):
        block = ((x + back_of(step, way, arriving) + NX) % NX) * NY + (y + far) % NY
        part = xbuf.at[a, b_rows(step, 2, way), aligned(block * PIECE, PIECE, PIECE)]
        index = (a, far, step - 1, way)
        return remote(part, part, bx_send.at[index], bx_recv.at[index], around(x_peers, way))

    def ax_move(a, step):
        for r in (1, 0):
            def act(r=r):
                for way in (0, 1):
                    if step:
                        ax_copy(a, r, step, way, True).wait_recv()
                    if step < 2:
                        ax_copy(a, r, step + 1, way, False).start()
                if step == 2:
                    for way in (0, 1):
                        a_copy(a, r, 1, way, False).start()
            when_active(r, act)

    def a_move(a, step):
        for r in (1, 0):
            def act(r=r):
                for way in (0, 1):
                    a_copy(a, r, step, way, True).wait_recv()
                    if step < 4:
                        a_copy(a, r, step + 1, way, False).start()
            when_active(r, act)

    def bx_start(a, *fars):
        for far in fars:
            for way in (0, 1):
                bx_copy(a, far % NY, 1, way, False).start()

    def bx_move(a, step, *fars):
        for far in fars:
            for way in (0, 1):
                bx_copy(a, far % NY, step, way, True).wait_recv()
                if step == 1:
                    bx_copy(a, far % NY, 2, way, False).start()

    def by_move(a, step):
        for way in (0, 1):
            by_copy(a, step, way, True).wait_recv()
            if step < 4:
                by_copy(a, step + 1, way, False).start()
        bx_start(a, *((-step, step) if step < 4 else (4,)))

    def round_of(a, number):
        if number == 0:
            for r in (2, 3):
                z_arrival(a, r).wait_recv()
            for way in (0, 1):
                by_copy(a, 1, way, False).start()
            bx_start(a, 0)
            for r in (1, 0):
                when_active(r, lambda r=r: z_arrival(a, r).wait_recv())
            ax_move(a, 0)
        elif number == 1:
            by_move(a, 1)
            ax_move(a, 1)
        elif number == 2:
            by_move(a, 2)
            ax_move(a, 2)
            bx_move(a, 1, 0)
        elif number == 3:
            by_move(a, 3)
            bx_move(a, 1, -1, 1)
        elif number == 4:
            by_move(a, 4)
            a_move(a, 1)
            bx_move(a, 1, -2, 2)
        elif number == 5:
            a_move(a, 2)
            bx_move(a, 1, -3, 3, 4)
            a_move(a, 3)
        else:
            bx_move(a, 2, 0, -1, 1, -2, 2, -3, 3, 4)
            a_move(a, 4)

    def pass_heads(a, distances):
        for s in distances:
            head_copy(a, s, True).wait_recv()
            share_copy(a, s, False).start()

    def finish_tokens(a):
        for s in range(NZ):
            share_copy(a, s, True).wait_recv()

        @pl.when(is_source)
        def _():
            own_tokens(a).wait()

    def drain_transfers(a):
        @pl.when(is_source)
        def _():
            for s in range(1, NZ):
                z_copy(a, s).wait_send()
        for s in range(1, NZ):
            head_copy(a, s, False).wait_send()
            if a == TRAIN:
                meta_copy(s, False).wait_send()
        for s in range(NZ):
            share_copy(a, s, False).wait_send()
        for way in (0, 1):
            for step in range(1, 5):
                by_copy(a, step, way, False).wait_send()
            for far in range(NY):
                for step in (1, 2):
                    bx_copy(a, far, step, way, False).wait_send()
        for r in (0, 1):
            def act(r=r):
                for way in (0, 1):
                    for step in (1, 2):
                        ax_copy(a, r, step, way, False).wait_send()
                    for step in range(1, 5):
                        a_copy(a, r, step, way, False).wait_send()
            when_active(r, act)

    def drain_home():
        for q in range(NZ):
            home_copy(q, False).wait_send()

    def send_tokens(a):
        @pl.when(is_source)
        def _():
            for s in (5, 2, 6, 1, 3, 7, 4):
                z_copy(a, s).start()
            own_tokens(a).start()

    def send_heads(a, distances):
        for s in distances:
            head_copy(a, s, False).start()

    send_tokens(TRAIN)
    own_meta.start()
    for s in range(1, NZ):
        meta_copy(s, False).start()
    own_rows(TRAIN).start()
    own_rows(REF).start()
    stats_t[0] = jnp.zeros((8, LANES), f32)
    stats_r[0] = jnp.zeros((16, LANES), f32)
    round_of(TRAIN, 0)
    send_heads(TRAIN, FAR_FIRST)
    round_of(TRAIN, 1)
    own_rows(TRAIN).wait()
    share_copy(TRAIN, 0, False).start()
    own_rows(REF).wait()
    share_copy(REF, 0, False).start()
    round_of(TRAIN, 2)
    for q in range(NZ):
        home_local(q).start()
        home_copy(q, False).start()
    round_of(TRAIN, 3)
    send_tokens(REF)
    send_heads(REF, (4, 1, 7))
    round_of(TRAIN, 4)
    round_of(TRAIN, 5)
    pass_heads(TRAIN, NEAR_FIRST)
    round_of(REF, 0)
    round_of(TRAIN, 6)
    round_of(REF, 1)
    own_meta.wait()
    for s in range(1, NZ):
        meta_copy(s, True).wait_recv()
    finish_tokens(TRAIN)

    row = lax.broadcasted_iota(jnp.int32, (BOTH, TOK), 0)
    within = row % ROWS
    chip = v // 2
    row_id = (2 * chip + row // ROWS) * 1008 + z * ROWS - 16 * (z // 7) + within
    valid = jnp.logical_or(within >= 16, z < 7)

    def hits(slot):
        target = lax.shift_right_logical(meta_all[4 * c + slot], 1)
        return jnp.logical_and(row_id == target, valid)

    def local_stats(a, slots):
        for r in slots:
            slot = (z + r) % 4
            table = lax.dot_general(
                gbuf[a], xbuf[a, TOK * r:TOK * (r + 1), :], LAST, preferred_element_type=f32
            )
            if a == TRAIN:
                logits[r] = table
            top = jnp.max(jnp.where(valid, table, -jnp.inf), axis=0, keepdims=True)
            parts = jnp.where(valid, jnp.exp(table - top), 0.0)
            picked = jnp.where(hits(slot), table, 0.0)
            mine = (stats_r, stats_t)[a]
            mine[0, pl.ds(slot, 1), :TOK] = top
            mine[0, pl.ds(4 + slot, 1), :TOK] = jnp.sum(parts, axis=0, keepdims=True)
            stats_r[0, pl.ds(8 + 4 * a + slot, 1), :TOK] = jnp.sum(picked, axis=0, keepdims=True)

    sums = (
        ((stats_r, zstat_r, xstat_r, ystat_r), both_r), ((stats_t, zstat_t, xstat_t, ystat_t), both_t)
    )
    hops = ((z_peers, tz_send, tz_recv), (x_peers, tx_send, tx_recv), (y_peers, ty_send, ty_recv))

    def stat_copies(a, level):
        peers, send, recv = hops[level]
        bufs = sums[a][0]
        return [
            remote(
                bufs[0].at[level], bufs[level + 1].at[s], send.at[a, s], recv.at[a, s], peers[s + 1]
            )
            for s in range(len(peers) - 1)
        ]

    def stat_send(a, level):
        for copy in stat_copies(a, level):
            copy.start()

    def stat_merge(a, level):
        bufs, result = sums[a]
        copies = stat_copies(a, level)
        for copy in copies:
            copy.wait_recv()
        blocks = [bufs[0][level]] + [bufs[level + 1][s] for s in range(len(copies))]
        top = functools.reduce(jnp.maximum, [b[0:4] for b in blocks])
        total = sum(b[4:8] * jnp.exp(b[0:4] - top) for b in blocks)
        merged = jnp.concatenate([top, total] + [sum(b[8:] for b in blocks)] * (1 - a), axis=0)
        if level < 2:
            bufs[0][level + 1] = merged
        else:
            result[c] = merged

    def stat_share(a, arriving):
        part = sums[a][1].at[1 - c if arriving else c]
        return remote(part, part, tc_send.at[a], tc_recv.at[a], sibling)

    def drain_stats(a):
        for level in range(3):
            for copy in stat_copies(a, level):
                copy.wait_send()
        stat_share(a, False).wait_send()

    local_stats(TRAIN, range(4))
    stat_send(TRAIN, 0)
    round_of(REF, 2)
    stat_merge(TRAIN, 0)
    stat_send(TRAIN, 1)
    send_heads(REF, (3, 5))
    round_of(REF, 3)
    stat_merge(TRAIN, 1)
    stat_send(TRAIN, 2)
    stat_merge(TRAIN, 2)
    stat_share(TRAIN, False).start()

    upper = (
        lax.broadcasted_iota(jnp.int32, (TOK, TOK), 0)
        <= lax.broadcasted_iota(jnp.int32, (TOK, TOK), 1)
    ).astype(jnp.bfloat16)
    place = lax.broadcasted_iota(jnp.int32, (SLOT, TOK), 0)

    def choose(weight, place):
        count = jnp.dot(
            jnp.broadcast_to(weight, (8, TOK)).astype(jnp.bfloat16), upper,
            preferred_element_type=f32,
        )[0:1].astype(jnp.int32)
        return jnp.logical_and(place == count - 1, weight != 0)

    def slopes(b):
        for slot in (2 * b, 2 * b + 1):
            pick = choose(meta_all[4 * c + slot] & 1, place).astype(jnp.bfloat16)
            top = both_t[c, slot:slot + 1, :TOK]
            total = both_t[c, 4 + slot:5 + slot, :TOK]
            share = jnp.exp(logits[(slot + 4 - z % 4) % 4] - top) / total
            slope = jnp.where(valid, loss_scale * (share - hits(slot).astype(f32)), 0.0)
            rows = lax.dot_general(
                pick, slope.astype(jnp.bfloat16), LAST, preferred_element_type=f32
            )
            start = SLOT * (slot - 2 * b)
            gathered[z, b, start:start + SLOT, :] = rows.astype(jnp.bfloat16)

    def e_copy(b, step, way, arriving):
        rows = pl.ds(0, PAIR) if step < 4 else pl.ds(SLOT * way, SLOT)
        part = gathered.at[(z + back_of(step, way, arriving) + NZ) % NZ, b, rows, :]
        index = (b, step - 1, way)
        return remote(part, part, ez_send.at[index], ez_recv.at[index], around(z_peers, way))

    def e_move(b, step):
        for way in (0, 1):
            if step:
                e_copy(b, step, way, True).wait_recv()
            if step < 4:
                e_copy(b, step + 1, way, False).start()

    def x_copy(b, s):
        return remote(
            grad.at[b, (x + s) % NX], xgrad.at[b, s - 1], gx_send.at[b, s - 1],
            gx_recv.at[b, s - 1], x_peers[s],
        )

    def turned_part(b, q):
        return turned.at[b, q // 4, aligned((q % 4) * 32, 32, 32), :]

    def y_copy(b, s):
        return remote(
            turned_part(b, (y + s) % NY), ygrad.at[b, s - 1], gy_send.at[b, s - 1],
            gy_recv.at[b, s - 1], y_peers[s],
        )

    def final_copy(b):
        return remote(
            summed.at[b], piece.at[aligned((y % 2) * 32, 32, 32), :], f_send.at[b],
            f_recv.at[y % 2], dests[b],
        )

    def final_stay(b):
        return pltpu.make_async_copy(
            summed.at[b], piece.at[aligned((y % 2) * 32, 32, 32), :], local_sem.at[5 + b]
        )

    def multiply(b):
        columns = jnp.concatenate([gathered[q, b] for q in range(NZ)], axis=1)
        for q in range(NX):
            grad[b, q] = jnp.dot(
                columns, home[:, 128 * q:128 * (q + 1)], preferred_element_type=f32
            )
        for s in (2, 1, 3):
            x_copy(b, s).start()

    def turn(b):
        for s in range(1, NX):
            x_copy(b, s).wait_recv()
        total = grad[b, x] + xgrad[b, 0] + xgrad[b, 1] + xgrad[b, 2]
        for i in (0, 1):
            block = jnp.concatenate(
                [total[SLOT * i:SLOT * (i + 1)], jnp.zeros((128 - SLOT, 128), f32)], axis=0
            )
            turned[b, i] = block.T
        for s in FAR_FIRST:
            y_copy(b, s).start()

    def hand_over(b):
        for s in range(1, NY):
            y_copy(b, s).wait_recv()
        summed[b] = turned_part(b, y)[...] + sum(ygrad[b, s] for s in range(NY - 1))

        @pl.when(jnp.logical_not(is_here(dests[b])))
        def _():
            final_copy(b).start()

        @pl.when(is_here(dests[b]))
        def _():
            final_stay(b).start()
            final_stay(b).wait()

    def drain_grads():
        for b in (0, 1):
            for way in (0, 1):
                for step in range(1, 5):
                    e_copy(b, step, way, False).wait_send()
            for s in range(1, NX):
                x_copy(b, s).wait_send()
            for s in range(1, NY):
                y_copy(b, s).wait_send()

            @pl.when(jnp.logical_not(is_here(dests[b])))
            def _():
                final_copy(b).wait_send()

    slopes(0)
    e_move(0, 0)
    slopes(1)
    e_move(1, 0)
    round_of(REF, 4)
    e_move(0, 1)
    e_move(1, 1)
    pass_heads(REF, (1, 7, 4))
    e_move(0, 2)
    e_move(1, 2)
    round_of(REF, 5)
    pass_heads(REF, (3, 5))
    e_move(0, 3)
    e_move(1, 3)
    send_heads(REF, (2, 6))
    for q in range(NZ):
        home_local(q).wait()
        home_copy(q, True).wait_recv()
    e_move(0, 4)
    multiply(0)
    e_move(1, 4)
    multiply(1)
    pass_heads(REF, (2, 6))
    round_of(REF, 6)
    finish_tokens(REF)
    local_stats(REF, range(4))
    stat_send(REF, 0)
    turn(0)
    turn(1)
    stat_merge(REF, 0)
    stat_send(REF, 1)
    hand_over(0)
    hand_over(1)
    stat_merge(REF, 1)
    stat_send(REF, 2)
    for h in (0, 1):
        @pl.when(jnp.logical_not(is_here(origins[h])))
        def _():
            part = piece.at[pl.ds(32 * h, 32), :]
            remote(part, part, f_send.at[0], f_recv.at[h], sibling).wait_recv()
    own_place = choose(
        meta_all[z] & 1, lax.broadcasted_iota(jnp.int32, (128, TOK), 0)
    ).astype(f32)
    grad_out[...] = jnp.dot(
        piece[...], own_place, precision=lax.Precision.HIGHEST, preferred_element_type=f32
    )
    stat_merge(REF, 2)
    stat_share(REF, False).start()
    for a in (TRAIN, REF):
        stat_share(a, True).wait_recv()

    def cross(a, h, first, count):
        block = sums[a][1].at[h]
        top = block[pl.ds(first, count), :TOK]
        total = block[pl.ds(4 + first, count), :TOK]
        return jnp.log(total) + top - both_r[h, pl.ds(8 + 4 * a + first, count), :TOK]

    excess_out[...] = cross(TRAIN, z // 4, z % 4, 1) - cross(REF, z // 4, z % 4, 1)
    loss = jnp.zeros((1, 1), f32)
    for h in (0, 1):
        weight = jnp.concatenate([meta_all[4 * h + i] & 1 for i in range(4)], axis=0)
        loss = loss + jnp.sum(
            weight.astype(f32) * cross(TRAIN, h, 0, 4), axis=(0, 1), keepdims=True
        )
    loss_out[...] = jnp.broadcast_to(loss / (NZ * SEL), loss_out.shape)

    for a in (REF, TRAIN):
        drain_transfers(a)
        drain_stats(a)
    drain_home()
    drain_grads()


def fused(hidden_ref, hidden_train, head_ref, head_train, targets, mask):
    anywhere = pl.BlockSpec(memory_space=pl.ANY)
    vmem = pl.BlockSpec(memory_space=pltpu.VMEM)
    dma = pltpu.SemaphoreType.DMA
    sds = jax.ShapeDtypeStruct
    f32, bf16 = jnp.float32, jnp.bfloat16
    buf = pltpu.VMEM
    pairs = [
        (2, NZ - 1), (2, 4), (NZ - 1,), (NZ - 1,), (2, NZ - 1), (2, NZ - 1), (2, NZ), (2, NZ),
        (NZ,), (NZ,), (NZ,), (2, 2, 2, 2), (2, 2, 2, 2), (2, 2, 4, 2), (2, 2, 4, 2), (2, 4, 2), (2, 4, 2),
        (2, NY, 2, 2), (2, NY, 2, 2),
        (2, NZ - 1), (2, NZ - 1), (2, NX - 1), (2, NX - 1), (2, NY - 1), (2, NY - 1), (2,), (2,),
        (2, 4, 2), (2, 4, 2), (2, NX - 1), (2, NX - 1), (2, NY - 1), (2, NY - 1), (2,), (2,),
    ]
    return pl.pallas_call(
        kernel,
        out_shape=[sds((64, TOK), f32), sds((1, TOK), f32), sds((1, 128), f32)],
        in_specs=[anywhere] * 4 + [vmem] * 2,
        out_specs=[vmem] * 3,
        scratch_shapes=[
            buf((1, TOK), jnp.int32), buf((NZ, 1, TOK), jnp.int32),
            *[
                buf((count, rows, LANES), f32)
                for rows in (8, 16) for count in (3, NZ - 1, NX - 1, NY - 1, 2)
            ],
            buf((2, 4 * TOK, WIDTH), bf16), buf((2, BOTH, WIDTH), bf16),
            buf((NZ * BOTH, FEAT), bf16), buf((4, BOTH, TOK), f32),
            buf((NZ, 2, PAIR, BOTH), bf16), buf((2, NX, PAIR, 128), f32),
            buf((2, NX - 1, PAIR, 128), f32), buf((2, 2, 128, 128), f32),
            buf((2, NY - 1, 32, 128), f32), buf((2, 32, 128), f32), buf((64, 128), f32),
            dma((7,)), *[dma(shape) for shape in pairs],
        ],
        compiler_params=pltpu.CompilerParams(
            collective_id=0, has_side_effects=True, vmem_limit_bytes=60 * 1024 * 1024
        ),
        name="fused",
    )(hidden_ref, hidden_train, head_ref, head_train, targets, mask)


def body(hidden_ref, hidden_train, head_ref, head_train, targets, mask):
    hidden_grad, excess, loss = fused(
        hidden_ref, hidden_train, head_ref, head_train,
        targets.reshape(1, TOK), mask.reshape(1, TOK),
    )
    return (excess.reshape(TOK), loss[0, 0], hidden_grad)


def solution(mesh):
    in_specs = (P("dp", None), P("dp", None), P("vocab", "dp"), P("vocab", "dp"), P("dp"), P("dp"))
    out_specs = (P("dp"), P(), P("vocab", "dp"))
    return jax.shard_map(body, mesh=mesh, in_specs=in_specs, out_specs=out_specs, check_vma=False)
```

```python
import functools

import jax
import jax.numpy as jnp
from jax import lax
from jax.experimental import pallas as pl
from jax.experimental.pallas import tpu as pltpu
from jax.sharding import PartitionSpec as P

MESH = pl.DeviceIdType.MESH
NX, NY, NZ = 4, 8, 8
loss_scale = 64.0
TOK = 160
SEL = 100
SLOT = 112
ROWS = 128
PIECE = 128
FEAT = 512
WIDTH = 4096
PAIR = 2 * SLOT
LANES = 256
BOTH = 2 * ROWS
FAR_FIRST = (4, 3, 5, 2, 6, 1, 7)
NEAR_FIRST = (1, 7, 2, 6, 3, 5, 4)
LAST = (((1,), (1,)), ((), ()))
REF, TRAIN = 0, 1


def coords():
    z = lax.axis_index("dp")
    v = lax.axis_index("vocab")
    return v // 16, (v // 2) % NY, z, v % 2


def vocab_index(x, y, c):
    return (x * NY + y) * 2 + c


def remote(src, dst, send_sem, recv_sem, device):
    return pltpu.make_async_remote_copy(
        src_ref=src, dst_ref=dst, send_sem=send_sem, recv_sem=recv_sem,
        device_id=device, device_id_type=MESH,
    )


def aligned(start, size, step):
    return pl.ds(pl.multiple_of(start, step), size)


def kernel(
    hid_ref, hid_train, head_ref, head_train, targets, mask,
    grad_out, excess_out, loss_out,
    meta, meta_all, stats_t, zstat_t, xstat_t, ystat_t, both_t,
    stats_r, zstat_r, xstat_r, ystat_r, both_r, xbuf, gbuf, home, logits, gathered, grad, xgrad, turned, ygrad, summed, piece,
    local_sem, z_send, z_recv, m_send, m_recv, w_send, w_recv, s_send, s_recv,
    h_local, h_send, h_recv, ax_send, ax_recv, ay_send, ay_recv, by_send, by_recv, bx_send, bx_recv,
    tz_send, tz_recv, tx_send, tx_recv, ty_send, ty_recv, tc_send, tc_recv,
    ez_send, ez_recv, gx_send, gx_recv, gy_send, gy_recv, f_send, f_recv,
):
    f32 = jnp.float32
    x, y, z, c = coords()
    v = vocab_index(x, y, c)
    sibling = (z, vocab_index(x, y, 1 - c))
    z_peers = [None] + [((z + s) % NZ, v) for s in range(1, NZ)]
    x_peers = [None] + [(z, vocab_index((x + s) % NX, y, c)) for s in range(1, NX)]
    y_peers = [None] + [(z, vocab_index(x, (y + s) % NY, c)) for s in range(1, NY)]
    dests = [(4 * c + 2 * b + y // 4, 8 * z + 2 * x + (y % 4) // 2) for b in (0, 1)]
    origins = [
        (v // 8, vocab_index((v % 8) // 2, 4 * (z % 2) + 2 * (v % 2) + h, z // 4)) for h in (0, 1)
    ]

    def is_here(device):
        return jnp.logical_and(device[0] == z, device[1] == v)

    barrier = pltpu.get_barrier_semaphore()
    friends = z_peers[1:] + x_peers[1:] + y_peers[1:] + [sibling]
    for device in friends:
        pl.semaphore_signal(barrier, inc=1, device_id=device, device_id_type=MESH)
    expected = len(friends) + 4
    for device in dests + origins:
        expected = expected - is_here(device).astype(jnp.int32)

        @pl.when(jnp.logical_not(is_here(device)))
        def _():
            pl.semaphore_signal(barrier, inc=1, device_id=device, device_id_type=MESH)

    pl.semaphore_wait(barrier, expected)

    meta[...] = 2 * targets[...] + mask[...]

    is_source = z // 4 == c
    hid = (hid_ref, hid_train)
    heads = (head_ref, head_train)

    def when_active(r, act):
        if r:
            act()
        else:
            pl.when(jnp.logical_not(is_source))(act)

    def z_columns(r):
        if r < 2:
            return aligned((y * NX + x) * PIECE, PIECE, PIECE)
        return aligned((x * NY + y) * PIECE, PIECE, PIECE)

    def z_copy(a, s):
        r = -s % 4
        columns = z_columns(r)
        return remote(
            hid[a].at[:, columns], xbuf.at[a, pl.ds(TOK * r, TOK), columns],
            z_send.at[a, s - 1], z_recv.at[a, r], z_peers[s],
        )

    def z_arrival(a, r):
        part = xbuf.at[a, pl.ds(TOK * r, TOK), z_columns(r)]
        return remote(part, part, z_send.at[a, 0], z_recv.at[a, r], sibling)

    def own_tokens(a):
        return pltpu.make_async_copy(hid[a], xbuf.at[a, pl.ds(0, TOK), :], local_sem.at[a])

    def meta_copy(s, arriving):
        source = (z + NZ - s) % NZ if arriving else z
        return remote(meta, meta_all.at[source], m_send.at[s - 1], m_recv.at[s - 1], z_peers[s])

    def row_block(q):
        return aligned(q * ROWS - 16 * (q // 7), ROWS, 16)

    def head_part(a, core, source):
        return gbuf.at[a, aligned(ROWS * core, ROWS, ROWS), aligned(source * FEAT, FEAT, FEAT)]

    def head_copy(a, s, arriving):
        source = (z + NZ - s) % NZ if arriving else z
        return remote(
            heads[a].at[row_block((z + s) % NZ), :], head_part(a, c, source),
            w_send.at[a, s - 1], w_recv.at[a, s - 1], z_peers[s],
        )

    def own_rows(a):
        return pltpu.make_async_copy(
            heads[a].at[row_block(z), :], head_part(a, c, z), local_sem.at[2 + a]
        )

    def share_copy(a, s, arriving):
        part = head_part(a, 1 - c if arriving else c, (z + NZ - s) % NZ)
        return remote(part, part, s_send.at[a, s], s_recv.at[a, s], sibling)

    own_meta = pltpu.make_async_copy(meta, meta_all.at[z], local_sem.at[4])

    def home_local(q):
        return pltpu.make_async_copy(
            head_train.at[row_block(q), :], home.at[aligned(q * BOTH + c * ROWS, ROWS, ROWS), :],
            h_local.at[q],
        )

    def home_copy(q, arriving):
        core = 1 - c if arriving else c
        return remote(
            head_train.at[row_block(q), :], home.at[aligned(q * BOTH + core * ROWS, ROWS, ROWS), :],
            h_send.at[q], h_recv.at[q], sibling,
        )

    def around(peers, way):
        return peers[1 if way == 0 else len(peers) - 1]

    def back_of(step, way, arriving):
        back = step if arriving else step - 1
        return -back if way == 0 else back

    def ax_copy(a, r, step, way, arriving):
        block = y * NX + (x + back_of(step, way, arriving) + NX) % NX
        rows = pl.ds(TOK * r, TOK) if step < 2 else pl.ds(TOK * r + 80 * way, 80)
        part = xbuf.at[a, rows, aligned(block * PIECE, PIECE, PIECE)]
        index = (a, r, step - 1, way)
        return remote(part, part, ax_send.at[index], ax_recv.at[index], around(x_peers, way))

    def a_copy(a, r, step, way, arriving):
        block = (y + back_of(step, way, arriving) + NY) % NY
        rows = pl.ds(TOK * r, TOK) if step < 4 else pl.ds(TOK * r + 80 * way, 80)
        part = xbuf.at[a, rows, aligned(block * FEAT, FEAT, FEAT)]
        index = (a, r, step - 1, way)
        return remote(part, part, ay_send.at[index], ay_recv.at[index], around(y_peers, way))

    def b_rows(step, last, way):
        return pl.ds(2 * TOK, 2 * TOK) if step < last else pl.ds(2 * TOK + TOK * way, TOK)

    def by_copy(a, step, way, arriving):
        block = x * NY + (y + back_of(step, way, arriving) + NY) % NY
        part = xbuf.at[a, b_rows(step, 4, way), aligned(block * PIECE, PIECE, PIECE)]
        index = (a, step - 1, way)
        return remote(part, part, by_send.at[index], by_recv.at[index], around(y_peers, way))

    def bx_copy(a, far, step, way, arriving):
        block = ((x + back_of(step, way, arriving) + NX) % NX) * NY + (y + far) % NY
        part = xbuf.at[a, b_rows(step, 2, way), aligned(block * PIECE, PIECE, PIECE)]
        index = (a, far, step - 1, way)
        return remote(part, part, bx_send.at[index], bx_recv.at[index], around(x_peers, way))

    def ax_move(a, step):
        for r in (1, 0):
            def act(r=r):
                for way in (0, 1):
                    if step:
                        ax_copy(a, r, step, way, True).wait_recv()
                    if step < 2:
                        ax_copy(a, r, step + 1, way, False).start()
                if step == 2:
                    for way in (0, 1):
                        a_copy(a, r, 1, way, False).start()
            when_active(r, act)

    def a_move(a, step):
        for r in (1, 0):
            def act(r=r):
                for way in (0, 1):
                    a_copy(a, r, step, way, True).wait_recv()
                    if step < 4:
                        a_copy(a, r, step + 1, way, False).start()
            when_active(r, act)

    def bx_start(a, *fars):
        for far in fars:
            for way in (0, 1):
                bx_copy(a, far % NY, 1, way, False).start()

    def bx_move(a, step, *fars):
        for far in fars:
            for way in (0, 1):
                bx_copy(a, far % NY, step, way, True).wait_recv()
                if step == 1:
                    bx_copy(a, far % NY, 2, way, False).start()

    def by_move(a, step):
        for way in (0, 1):
            by_copy(a, step, way, True).wait_recv()
            if step < 4:
                by_copy(a, step + 1, way, False).start()
        bx_start(a, *((-step, step) if step < 4 else (4,)))

    def round_of(a, number):
        if number == 0:
            for r in (2, 3):
                z_arrival(a, r).wait_recv()
            for way in (0, 1):
                by_copy(a, 1, way, False).start()
            bx_start(a, 0)
            for r in (1, 0):
                when_active(r, lambda r=r: z_arrival(a, r).wait_recv())
            ax_move(a, 0)
        elif number == 1:
            by_move(a, 1)
            ax_move(a, 1)
        elif number == 2:
            by_move(a, 2)
            ax_move(a, 2)
            bx_move(a, 1, 0)
        elif number == 3:
            by_move(a, 3)
            bx_move(a, 1, -1, 1)
        elif number == 4:
            by_move(a, 4)
            a_move(a, 1)
            bx_move(a, 1, -2, 2)
        elif number == 5:
            a_move(a, 2)
            bx_move(a, 1, -3, 3, 4)
            a_move(a, 3)
        else:
            bx_move(a, 2, 0, -1, 1, -2, 2, -3, 3, 4)
            a_move(a, 4)

    def pass_heads(a, distances):
        for s in distances:
            head_copy(a, s, True).wait_recv()
            share_copy(a, s, False).start()

    def finish_tokens(a):
        for s in range(NZ):
            share_copy(a, s, True).wait_recv()

        @pl.when(is_source)
        def _():
            own_tokens(a).wait()

    def drain_transfers(a):
        @pl.when(is_source)
        def _():
            for s in range(1, NZ):
                z_copy(a, s).wait_send()
        for s in range(1, NZ):
            head_copy(a, s, False).wait_send()
            if a == TRAIN:
                meta_copy(s, False).wait_send()
        for s in range(NZ):
            share_copy(a, s, False).wait_send()
        for way in (0, 1):
            for step in range(1, 5):
                by_copy(a, step, way, False).wait_send()
            for far in range(NY):
                for step in (1, 2):
                    bx_copy(a, far, step, way, False).wait_send()
        for r in (0, 1):
            def act(r=r):
                for way in (0, 1):
                    for step in (1, 2):
                        ax_copy(a, r, step, way, False).wait_send()
                    for step in range(1, 5):
                        a_copy(a, r, step, way, False).wait_send()
            when_active(r, act)

    def drain_home():
        for q in range(NZ):
            home_copy(q, False).wait_send()

    def send_tokens(a):
        @pl.when(is_source)
        def _():
            for s in (5, 2, 6, 1, 3, 7, 4):
                z_copy(a, s).start()
            own_tokens(a).start()

    def send_heads(a, distances):
        for s in distances:
            head_copy(a, s, False).start()

    send_tokens(TRAIN)
    own_meta.start()
    for s in range(1, NZ):
        meta_copy(s, False).start()
    own_rows(TRAIN).start()
    own_rows(REF).start()
    stats_t[0] = jnp.zeros((8, LANES), f32)
    stats_r[0] = jnp.zeros((16, LANES), f32)
    round_of(TRAIN, 0)
    send_heads(TRAIN, FAR_FIRST)
    round_of(TRAIN, 1)
    own_rows(TRAIN).wait()
    share_copy(TRAIN, 0, False).start()
    own_rows(REF).wait()
    share_copy(REF, 0, False).start()
    round_of(TRAIN, 2)
    for q in range(NZ):
        home_local(q).start()
        home_copy(q, False).start()
    round_of(TRAIN, 3)
    send_tokens(REF)
    send_heads(REF, (4, 1, 7))
    round_of(TRAIN, 4)
    round_of(TRAIN, 5)
    pass_heads(TRAIN, NEAR_FIRST)
    round_of(REF, 0)
    round_of(TRAIN, 6)
    round_of(REF, 1)
    own_meta.wait()
    for s in range(1, NZ):
        meta_copy(s, True).wait_recv()
    finish_tokens(TRAIN)

    row = lax.broadcasted_iota(jnp.int32, (BOTH, TOK), 0)
    within = row % ROWS
    chip = v // 2
    row_id = (2 * chip + row // ROWS) * 1008 + z * ROWS - 16 * (z // 7) + within
    valid = jnp.logical_or(within >= 16, z < 7)

    def hits(slot):
        target = lax.shift_right_logical(meta_all[4 * c + slot], 1)
        return jnp.logical_and(row_id == target, valid)

    def local_stats(a, slots):
        for r in slots:
            slot = (z + r) % 4
            table = lax.dot_general(
                gbuf[a], xbuf[a, TOK * r:TOK * (r + 1), :], LAST, preferred_element_type=f32
            )
            if a == TRAIN:
                logits[r] = table
            top = jnp.max(jnp.where(valid, table, -jnp.inf), axis=0, keepdims=True)
            parts = jnp.where(valid, jnp.exp(table - top), 0.0)
            picked = jnp.where(hits(slot), table, 0.0)
            mine = (stats_r, stats_t)[a]
            mine[0, pl.ds(slot, 1), :TOK] = top
            mine[0, pl.ds(4 + slot, 1), :TOK] = jnp.sum(parts, axis=0, keepdims=True)
            stats_r[0, pl.ds(8 + 4 * a + slot, 1), :TOK] = jnp.sum(picked, axis=0, keepdims=True)

    sums = (
        ((stats_r, zstat_r, xstat_r, ystat_r), both_r), ((stats_t, zstat_t, xstat_t, ystat_t), both_t)
    )
    hops = ((z_peers, tz_send, tz_recv), (x_peers, tx_send, tx_recv), (y_peers, ty_send, ty_recv))

    def stat_copies(a, level):
        peers, send, recv = hops[level]
        bufs = sums[a][0]
        return [
            remote(
                bufs[0].at[level], bufs[level + 1].at[s], send.at[a, s], recv.at[a, s], peers[s + 1]
            )
            for s in range(len(peers) - 1)
        ]

    def stat_send(a, level):
        for copy in stat_copies(a, level):
            copy.start()

    def stat_merge(a, level):
        bufs, result = sums[a]
        copies = stat_copies(a, level)
        for copy in copies:
            copy.wait_recv()
        blocks = [bufs[0][level]] + [bufs[level + 1][s] for s in range(len(copies))]
        top = functools.reduce(jnp.maximum, [b[0:4] for b in blocks])
        total = sum(b[4:8] * jnp.exp(b[0:4] - top) for b in blocks)
        merged = jnp.concatenate([top, total] + [sum(b[8:] for b in blocks)] * (1 - a), axis=0)
        if level < 2:
            bufs[0][level + 1] = merged
        else:
            result[c] = merged

    def stat_share(a, arriving):
        part = sums[a][1].at[1 - c if arriving else c]
        return remote(part, part, tc_send.at[a], tc_recv.at[a], sibling)

    def drain_stats(a):
        for level in range(3):
            for copy in stat_copies(a, level):
                copy.wait_send()
        stat_share(a, False).wait_send()

    local_stats(TRAIN, range(4))
    stat_send(TRAIN, 0)
    round_of(REF, 2)
    stat_merge(TRAIN, 0)
    stat_send(TRAIN, 1)
    send_heads(REF, (3, 5))
    round_of(REF, 3)
    stat_merge(TRAIN, 1)
    stat_send(TRAIN, 2)
    stat_merge(TRAIN, 2)
    stat_share(TRAIN, False).start()

    upper = (
        lax.broadcasted_iota(jnp.int32, (TOK, TOK), 0)
        <= lax.broadcasted_iota(jnp.int32, (TOK, TOK), 1)
    ).astype(jnp.bfloat16)
    place = lax.broadcasted_iota(jnp.int32, (SLOT, TOK), 0)

    def choose(weight, place):
        count = jnp.dot(
            jnp.broadcast_to(weight, (8, TOK)).astype(jnp.bfloat16), upper,
            preferred_element_type=f32,
        )[0:1].astype(jnp.int32)
        return jnp.logical_and(place == count - 1, weight != 0)

    def slopes(b):
        for slot in (2 * b, 2 * b + 1):
            pick = choose(meta_all[4 * c + slot] & 1, place).astype(jnp.bfloat16)
            top = both_t[c, slot:slot + 1, :TOK]
            total = both_t[c, 4 + slot:5 + slot, :TOK]
            share = jnp.exp(logits[(slot + 4 - z % 4) % 4] - top) / total
            slope = jnp.where(valid, loss_scale * (share - hits(slot).astype(f32)), 0.0)
            rows = lax.dot_general(
                pick, slope.astype(jnp.bfloat16), LAST, preferred_element_type=f32
            )
            start = SLOT * (slot - 2 * b)
            gathered[z, b, start:start + SLOT, :] = rows.astype(jnp.bfloat16)

    def e_copy(b, step, way, arriving):
        rows = pl.ds(0, PAIR) if step < 4 else pl.ds(SLOT * way, SLOT)
        part = gathered.at[(z + back_of(step, way, arriving) + NZ) % NZ, b, rows, :]
        index = (b, step - 1, way)
        return remote(part, part, ez_send.at[index], ez_recv.at[index], around(z_peers, way))

    def e_move(b, step):
        for way in (0, 1):
            if step:
                e_copy(b, step, way, True).wait_recv()
            if step < 4:
                e_copy(b, step + 1, way, False).start()

    def x_copy(b, s):
        return remote(
            grad.at[b, (x + s) % NX], xgrad.at[b, s - 1], gx_send.at[b, s - 1],
            gx_recv.at[b, s - 1], x_peers[s],
        )

    def turned_part(b, q):
        return turned.at[b, q // 4, aligned((q % 4) * 32, 32, 32), :]

    def y_copy(b, s):
        return remote(
            turned_part(b, (y + s) % NY), ygrad.at[b, s - 1], gy_send.at[b, s - 1],
            gy_recv.at[b, s - 1], y_peers[s],
        )

    def final_copy(b):
        return remote(
            summed.at[b], piece.at[aligned((y % 2) * 32, 32, 32), :], f_send.at[b],
            f_recv.at[y % 2], dests[b],
        )

    def final_stay(b):
        return pltpu.make_async_copy(
            summed.at[b], piece.at[aligned((y % 2) * 32, 32, 32), :], local_sem.at[5 + b]
        )

    def multiply(b):
        columns = jnp.concatenate([gathered[q, b] for q in range(NZ)], axis=1)
        for q in range(NX):
            grad[b, q] = jnp.dot(
                columns, home[:, 128 * q:128 * (q + 1)], preferred_element_type=f32
            )
        for s in (2, 1, 3):
            x_copy(b, s).start()

    def turn(b):
        for s in range(1, NX):
            x_copy(b, s).wait_recv()
        total = grad[b, x] + xgrad[b, 0] + xgrad[b, 1] + xgrad[b, 2]
        for i in (0, 1):
            block = jnp.concatenate(
                [total[SLOT * i:SLOT * (i + 1)], jnp.zeros((128 - SLOT, 128), f32)], axis=0
            )
            turned[b, i] = block.T
        for s in FAR_FIRST:
            y_copy(b, s).start()

    def hand_over(b):
        for s in range(1, NY):
            y_copy(b, s).wait_recv()
        summed[b] = turned_part(b, y)[...] + sum(ygrad[b, s] for s in range(NY - 1))

        @pl.when(jnp.logical_not(is_here(dests[b])))
        def _():
            final_copy(b).start()

        @pl.when(is_here(dests[b]))
        def _():
            final_stay(b).start()
            final_stay(b).wait()

    def drain_grads():
        for b in (0, 1):
            for way in (0, 1):
                for step in range(1, 5):
                    e_copy(b, step, way, False).wait_send()
            for s in range(1, NX):
                x_copy(b, s).wait_send()
            for s in range(1, NY):
                y_copy(b, s).wait_send()

            @pl.when(jnp.logical_not(is_here(dests[b])))
            def _():
                final_copy(b).wait_send()

    slopes(0)
    e_move(0, 0)
    slopes(1)
    e_move(1, 0)
    round_of(REF, 4)
    e_move(0, 1)
    e_move(1, 1)
    pass_heads(REF, (1, 7, 4))
    e_move(0, 2)
    e_move(1, 2)
    round_of(REF, 5)
    pass_heads(REF, (3, 5))
    e_move(0, 3)
    e_move(1, 3)
    send_heads(REF, (2, 6))
    for q in range(NZ):
        home_local(q).wait()
        home_copy(q, True).wait_recv()
    drain_transfers(TRAIN)
    drain_stats(TRAIN)
    drain_home()
    e_move(0, 4)
    multiply(0)
    e_move(1, 4)
    multiply(1)
    pass_heads(REF, (2, 6))
    round_of(REF, 6)
    finish_tokens(REF)
    local_stats(REF, range(4))
    stat_send(REF, 0)
    turn(0)
    turn(1)
    stat_merge(REF, 0)
    stat_send(REF, 1)
    hand_over(0)
    hand_over(1)
    stat_merge(REF, 1)
    stat_send(REF, 2)
    drain_transfers(REF)
    for h in (0, 1):
        @pl.when(jnp.logical_not(is_here(origins[h])))
        def _():
            part = piece.at[pl.ds(32 * h, 32), :]
            remote(part, part, f_send.at[0], f_recv.at[h], sibling).wait_recv()
    own_place = choose(
        meta_all[z] & 1, lax.broadcasted_iota(jnp.int32, (128, TOK), 0)
    ).astype(f32)
    grad_out[...] = jnp.dot(
        piece[...], own_place, precision=lax.Precision.HIGHEST, preferred_element_type=f32
    )
    stat_merge(REF, 2)
    stat_share(REF, False).start()
    for a in (TRAIN, REF):
        stat_share(a, True).wait_recv()

    def cross(a, h, first, count):
        block = sums[a][1].at[h]
        top = block[pl.ds(first, count), :TOK]
        total = block[pl.ds(4 + first, count), :TOK]
        return jnp.log(total) + top - both_r[h, pl.ds(8 + 4 * a + first, count), :TOK]

    excess_out[...] = cross(TRAIN, z // 4, z % 4, 1) - cross(REF, z // 4, z % 4, 1)
    loss = jnp.zeros((1, 1), f32)
    for h in (0, 1):
        weight = jnp.concatenate([meta_all[4 * h + i] & 1 for i in range(4)], axis=0)
        loss = loss + jnp.sum(
            weight.astype(f32) * cross(TRAIN, h, 0, 4), axis=(0, 1), keepdims=True
        )
    loss_out[...] = jnp.broadcast_to(loss / (NZ * SEL), loss_out.shape)

    drain_stats(REF)
    drain_grads()


def fused(hidden_ref, hidden_train, head_ref, head_train, targets, mask):
    anywhere = pl.BlockSpec(memory_space=pl.ANY)
    vmem = pl.BlockSpec(memory_space=pltpu.VMEM)
    dma = pltpu.SemaphoreType.DMA
    sds = jax.ShapeDtypeStruct
    f32, bf16 = jnp.float32, jnp.bfloat16
    buf = pltpu.VMEM
    pairs = [
        (2, NZ - 1), (2, 4), (NZ - 1,), (NZ - 1,), (2, NZ - 1), (2, NZ - 1), (2, NZ), (2, NZ),
        (NZ,), (NZ,), (NZ,), (2, 2, 2, 2), (2, 2, 2, 2), (2, 2, 4, 2), (2, 2, 4, 2), (2, 4, 2), (2, 4, 2),
        (2, NY, 2, 2), (2, NY, 2, 2),
        (2, NZ - 1), (2, NZ - 1), (2, NX - 1), (2, NX - 1), (2, NY - 1), (2, NY - 1), (2,), (2,),
        (2, 4, 2), (2, 4, 2), (2, NX - 1), (2, NX - 1), (2, NY - 1), (2, NY - 1), (2,), (2,),
    ]
    return pl.pallas_call(
        kernel,
        out_shape=[sds((64, TOK), f32), sds((1, TOK), f32), sds((1, 128), f32)],
        in_specs=[anywhere] * 4 + [vmem] * 2,
        out_specs=[vmem] * 3,
        scratch_shapes=[
            buf((1, TOK), jnp.int32), buf((NZ, 1, TOK), jnp.int32),
            *[
                buf((count, rows, LANES), f32)
                for rows in (8, 16) for count in (3, NZ - 1, NX - 1, NY - 1, 2)
            ],
            buf((2, 4 * TOK, WIDTH), bf16), buf((2, BOTH, WIDTH), bf16),
            buf((NZ * BOTH, FEAT), bf16), buf((4, BOTH, TOK), f32),
            buf((NZ, 2, PAIR, BOTH), bf16), buf((2, NX, PAIR, 128), f32),
            buf((2, NX - 1, PAIR, 128), f32), buf((2, 2, 128, 128), f32),
            buf((2, NY - 1, 32, 128), f32), buf((2, 32, 128), f32), buf((64, 128), f32),
            dma((7,)), *[dma(shape) for shape in pairs],
        ],
        compiler_params=pltpu.CompilerParams(
            collective_id=0, has_side_effects=True, vmem_limit_bytes=60 * 1024 * 1024
        ),
        name="fused",
    )(hidden_ref, hidden_train, head_ref, head_train, targets, mask)


def body(hidden_ref, hidden_train, head_ref, head_train, targets, mask):
    hidden_grad, excess, loss = fused(
        hidden_ref, hidden_train, head_ref, head_train,
        targets.reshape(1, TOK), mask.reshape(1, TOK),
    )
    return (excess.reshape(TOK), loss[0, 0], hidden_grad)


def solution(mesh):
    in_specs = (P("dp", None), P("dp", None), P("vocab", "dp"), P("vocab", "dp"), P("dp"), P("dp"))
    out_specs = (P("dp"), P(), P("vocab", "dp"))
    return jax.shard_map(body, mesh=mesh, in_specs=in_specs, out_specs=out_specs, check_vma=False)
```
